32 devices in a mesh: clip: 2 (over y), tile: 4 (over z), slab: 2 (over x), chan: 2 (over core).
Axes of the slice: x: 2, y: 2, z: 4, core: 2. Of those that a mesh axis runs over, the one named last changes fastest.
Arguments:
- video: bfloat16 [16, 16, 128, 128], P(('clip', 'slab'), 'tile'), parts along dimension 0, may hold values from -6 to 6
- first_weight: bfloat16 [3, 3, 3, 128, 128], P(None, None, None, None, 'chan'), may hold values from -0.109375 to 0.109375
- first_bias: float32 [128], P('chan'), may hold values from -3 to 3
- second_weight: bfloat16 [3, 3, 3, 128, 256], replicated, may hold values from -0.109375 to 0.109375
- second_bias: float32 [256], P('chan'), may hold values from -3 to 3
Outputs:
- latents: bfloat16 [8, 16, 128, 256], P(('clip', 'slab'), 'tile', None, 'chan'), parts along dimension 0
The draws below stay inside these ranges and needn't reach their ends.
There are 2 independent parts, one for each index of `clip`. The reference program is written for one: setup_inputs(seed, part) draws one part's arguments, and reference() takes and returns one part's arrays. A program takes and returns all parts, laid end to end along the dimension named above; an argument that names none is the same for every part. Nothing has to cross between parts.
All inputs are finite; a program needn't handle non-finite values.
Results may differ from the reference program's by a relative error of at most 0.0095.
Values may be sent and summed in bfloat16 or wider, within the bound.
No kernel may reach another device: no remote copies, remote signals or barrier semaphores. Data moves between devices by JAX's collectives and lax.ppermute only.
A program may use at most 64 MiB of HBM per device.

```python
import jax
import jax.numpy as jnp
from jax import lax

CH_IN = 128
CH_MID = 128
CH_OUT = 256
W = 128
FRAMES = 8
HEIGHT = 16


def level_of(stream_key, shape, cuts, smallest, largest):
    def one(dim, parts):
        heights = jax.random.uniform(jax.random.fold_in(jax.random.fold_in(stream_key, 6), dim), (parts,), jnp.float32, smallest / len(cuts), largest / len(cuts))
        return jnp.repeat(jnp.exp(heights), shape[dim] // parts).reshape((-1,) + (1,) * (len(shape) - dim - 1))

    level = one(*cuts[0])
    for cut in cuts[1:]:
        level = level * one(*cut)
    return level


def scatter_about(rng, shape, spread, limit, shards=(), dtype=jnp.bfloat16):
    factor_of = level_of(rng, shape, shards, -0.22, 0.18) if shards else 1.0
    entries = jax.random.normal(rng, shape, jnp.float32) * spread * factor_of
    return jnp.minimum(jnp.maximum(entries, -limit), limit).astype(dtype)


def setup_inputs(seed: int = 0, part: int = 0) -> dict:
    arg_keys = jax.random.split(jax.random.key(seed), 6)
    part_keys = jax.random.split(jax.random.fold_in(arg_keys[5], part), 6)
    video = scatter_about(part_keys[0], (FRAMES, HEIGHT, W, CH_IN), 1.0, 6.0, ((0, 2), (1, 4)))
    first_weight = scatter_about(arg_keys[1], (3, 3, 3, CH_IN, CH_MID), (27 * CH_IN) ** -0.5, 0.109375, ((4, 2),))
    first_bias = scatter_about(arg_keys[2], (CH_MID,), 0.5, 3.0, ((0, 2),), jnp.float32)
    second_weight = scatter_about(arg_keys[3], (3, 3, 3, CH_MID, CH_OUT), (27 * CH_MID) ** -0.5, 0.109375)
    second_bias = scatter_about(arg_keys[4], (CH_OUT,), 0.5, 3.0, ((0, 2),), jnp.float32)
    return {"video": video, "first_weight": first_weight, "first_bias": first_bias, "second_weight": second_weight, "second_bias": second_bias}


def causal_convolve(source, kernel, stride):
    result = lax.conv_general_dilated(source[None], kernel, window_strides=(stride, 1, 1), padding=((2, 0), (1, 1), (1, 1)), dimension_numbers=("NDHWC", "DHWIO", "NDHWC"), preferred_element_type=jnp.float32)
    return result[0]


def reference(video, first_weight, first_bias, second_weight, second_bias):
    hidden = jax.nn.silu(causal_convolve(video, first_weight, 1) + first_bias).astype(jnp.bfloat16)
    return jax.nn.silu(causal_convolve(hidden, second_weight, 2) + second_bias).astype(jnp.bfloat16)
```

```python
import functools

import jax
import jax.numpy as jnp
from jax import lax
from jax.experimental import pallas as pl
from jax.experimental.pallas import tpu as pltpu
from jax.sharding import PartitionSpec as P

VMEM = pl.BlockSpec(memory_space=pltpu.VMEM)
ANY = pl.BlockSpec(memory_space=pl.ANY)
LIMIT = 48 * 1024 * 1024


def silu(value):
    return value / (1.0 + jnp.exp(-value))


def shifted_sum(parts, columns):
    size = parts[0].shape[0]
    cell = lax.broadcasted_iota(jnp.int32, parts[0].shape, 0) % columns
    low = jnp.where(cell == 0, 0.0, pltpu.roll(parts[0], 1, 0))
    high = jnp.where(cell == columns - 1, 0.0, pltpu.roll(parts[2], size - 1, 0))
    return parts[1] + low + high


def side():
    core = lax.axis_index("chan")
    return core, 2 * (1 - core), 2 * core


def border_known():
    core, tile = lax.axis_index("chan"), lax.axis_index("tile")
    last = lax.axis_size("tile") - 1
    return jnp.logical_not(jnp.logical_or((core == 0) & (tile == 0), (core == 1) & (tile == last)))


def pack_kernel(own, other, packed):
    core = lax.axis_index("chan")
    taps = own.shape[0]
    width = own.shape[3]
    for a in range(taps):
        for e in range(taps):
            full = []
            for b in range(taps):
                mine, theirs = own[a, b, e], other[a, b, e]
                left = jnp.where(core == 0, mine, theirs)
                right = jnp.where(core == 0, theirs, mine)
                full.append(jnp.concatenate([left, right], axis=1))
            nothing = jnp.zeros_like(full[0])
            for i in range(taps + 1):
                pair = [full[i - j] if 0 <= i - j < taps else nothing for j in range(2)]
                packed[
                    (a * (taps + 1) + i) * width : (a * (taps + 1) + i + 1) * width,
                    e * 2 * width : (e + 1) * 2 * width,
                ] = jnp.concatenate(pair, axis=1)


def first_layer(stack, start, frames, packed, bias):
    rows, columns, width = stack.shape[1:]
    taps = 3
    left = jnp.concatenate(
        [
            stack[start + a : start + a + frames, i].reshape(frames * columns, width)
            for a in range(taps)
            for i in range(rows)
        ],
        axis=1,
    )
    double = packed.shape[1] // taps
    parts = [
        jnp.dot(left, packed[:, e * double : (e + 1) * double], preferred_element_type=jnp.float32)
        for e in range(taps)
    ]
    return silu(shifted_sum(parts, columns) + bias).astype(jnp.bfloat16)


def whole_bias(core, own, other):
    return jnp.where(
        core == 0,
        jnp.concatenate([own[...], other[...]], axis=1),
        jnp.concatenate([other[...], own[...]], axis=1),
    )


def run_copies(copies):
    for copy in copies:
        copy.start()
    for copy in copies:
        copy.wait()


def inner_kernel(video, beyond, passed, passed_other, packed, bias_own, bias_other, hidden, stack, edge, sems):
    core, mine, over = side()
    slab = lax.axis_index("slab")
    known = border_known()
    frames = video.shape[0]
    extra = edge.shape[0]
    half = beyond.shape[1]
    columns = video.shape[2]

    always = [
        pltpu.make_async_copy(video.at[0:extra], stack.at[frames : frames + extra], sems.at[0]),
        pltpu.make_async_copy(
            video.at[0:extra, pl.ds(core * half, half)], edge.at[:, pl.ds(mine, half)], sems.at[1]
        ),
    ]
    earlier = [
        pltpu.make_async_copy(passed, stack.at[0:frames, pl.ds(core * half, half)], sems.at[2]),
        pltpu.make_async_copy(
            passed_other, stack.at[0:frames, pl.ds((1 - core) * half, half)], sems.at[3]
        ),
    ]
    border = pltpu.make_async_copy(beyond.at[0:extra], edge.at[:, pl.ds(over, half)], sems.at[4])
    for copy in always:
        copy.start()

    @pl.when(slab > 0)
    def _():
        run_copies(earlier)

    @pl.when(slab == 0)
    def _():
        stack[0:frames] = jnp.zeros((frames,) + stack.shape[1:], stack.dtype)

    @pl.when(known)
    def _():
        run_copies([border])

    @pl.when(jnp.logical_not(known))
    def _():
        edge[:, pl.ds(over, half)] = jnp.zeros((extra, half) + edge.shape[2:], edge.dtype)

    for copy in always:
        copy.wait()

    bias = whole_bias(core, bias_own, bias_other)
    bias = jnp.concatenate([bias, bias], axis=1)
    count = hidden.shape[0]
    width = hidden.shape[3]
    inner = first_layer(stack, 0, count, packed, bias).reshape(count, columns, 2 * width)
    for n in range(count):
        for j in range(2):
            row = inner[n, :, j * width : (j + 1) * width]
            if n < count - extra:
                row = jnp.where(slab > 0, row, jnp.zeros_like(row))
            hidden[n, mine + j] = row
    outer = first_layer(edge, 0, 1, packed, bias)
    for j in range(2):
        row = outer[:, j * width : (j + 1) * width]
        inside = known | (core != j)
        hidden[count - 1, over + j] = jnp.where(inside, row, jnp.zeros_like(row))


def outer_kernel(
    own, beyond, passed, passed_beyond, started, packed, second, bias_own, bias_other, out_own, out_other,
    latents, given, hidden, edge, sems,
):
    core, mine, over = side()
    slab = lax.axis_index("slab")
    known = border_known()
    frames, half, columns, width = own.shape
    late = edge.shape[0] - frames
    count = hidden.shape[0]

    begun = pltpu.make_async_copy(started, hidden, sems.at[0])
    always = [
        pltpu.make_async_copy(own.at[0:late], edge.at[frames : frames + late, pl.ds(mine, half)], sems.at[1])
    ]
    earlier = [pltpu.make_async_copy(passed, edge.at[0:frames, pl.ds(mine, half)], sems.at[2])]
    border = [
        pltpu.make_async_copy(beyond.at[0:late], edge.at[frames : frames + late, pl.ds(over, half)], sems.at[3])
    ]
    corner = [pltpu.make_async_copy(passed_beyond, edge.at[0:frames, pl.ds(over, half)], sems.at[4])]
    begun.start()
    for copy in always:
        copy.start()

    @pl.when(slab > 0)
    def _():
        run_copies(earlier)

    @pl.when(slab == 0)
    def _():
        edge[0:frames] = jnp.zeros((frames,) + edge.shape[1:], edge.dtype)

    @pl.when(known)
    def _():
        run_copies(border)

    @pl.when(known & (slab > 0))
    def _():
        run_copies(corner)

    @pl.when(jnp.logical_not(known))
    def _():
        edge[:, pl.ds(over, half)] = jnp.zeros((edge.shape[0], half) + edge.shape[2:], edge.dtype)

    for copy in always:
        copy.wait()
    begun.wait()

    bias = whole_bias(core, bias_own, bias_other)
    bias = jnp.concatenate([bias, bias], axis=1)
    outer = first_layer(edge, 0, count - 1, packed, bias).reshape(count - 1, columns, 2 * width)
    for n in range(count - 1):
        for j in range(2):
            row = outer[n, :, j * width : (j + 1) * width]
            inside = known | (core != j)
            if n < 2:
                inside = inside & (slab > 0)
            hidden[n, over + j] = jnp.where(inside, row, jnp.zeros_like(row))

    taps = second.shape[0]
    results = given.shape[0]
    left = jnp.concatenate(
        [
            jnp.concatenate(
                [hidden[2 * t + a, b : b + half].reshape(half * columns, width) for t in range(results)], axis=0
            )
            for a in range(taps)
            for b in range(taps)
        ],
        axis=1,
    )
    parts = [
        jnp.dot(
            left,
            jnp.concatenate([second[a, b, e] for a in range(taps) for b in range(taps)], axis=0),
            preferred_element_type=jnp.float32,
        )
        for e in range(taps)
    ]
    total = silu(shifted_sum(parts, columns) + whole_bias(core, out_own, out_other)).astype(jnp.bfloat16)
    portion = given.shape[3]
    total = total.reshape(results, half, columns, 2 * portion)
    low, high = total[..., :portion], total[..., portion:]
    latents[:, pl.ds(core * half, half)] = jnp.where(core == 0, low, high)
    given[...] = jnp.where(core == 0, high, low)


def cycle(value, axis):
    count = lax.axis_size(axis)
    return lax.ppermute(value, axis, [(i, (i + 1) % count) for i in range(count)])


def across_border(value):
    clips, tiles = lax.axis_size("clip"), lax.axis_size("tile")
    pairs = []
    for clip in range(clips):
        at = lambda c, t, k: (c * tiles + t) * 2 + k
        for tile in range(tiles - 1):
            pairs.append((at(clip, tile, 1), at(clip, tile + 1, 0)))
            pairs.append((at(clip, tile + 1, 0), at(clip, tile, 1)))
        if clips > 1:
            pairs.append((at(clip, 0, 0), at((clip + 1) % clips, 0, 0)))
            pairs.append((at(clip, tiles - 1, 1), at((clip + 1) % clips, tiles - 1, 1)))
    return lax.ppermute(value, ("clip", "tile", "chan"), pairs)


def params():
    return pltpu.CompilerParams(vmem_limit_bytes=LIMIT)


def shards(video, first_weight, first_bias, second_weight, second_bias):
    frames, rows, columns, width = video.shape
    half = rows // 2
    taps = first_weight.shape[0]
    assert half == taps - 1 and frames == 2 * (taps - 1) and lax.axis_size("chan") == 2
    core = lax.axis_index("chan")
    bf16 = jnp.bfloat16
    own = lax.dynamic_slice_in_dim(video, core * half, half, 1)
    beyond = across_border(own)
    passed = cycle(own, "slab")
    first_other = cycle(first_weight, "chan")
    bias_other = cycle(first_bias, "chan")
    out_other = cycle(second_bias, "chan")
    passed_beyond = cycle(beyond, "slab")
    passed_other = cycle(passed, "chan")

    packed = pl.pallas_call(
        pack_kernel,
        out_shape=jax.ShapeDtypeStruct((taps * (taps + 1) * width, taps * 2 * width), bf16),
        in_specs=[VMEM] * 2,
        out_specs=VMEM,
        compiler_params=params(),
        name="pack",
    )(first_weight, first_other)
    line = lambda v: v.reshape(1, -1)
    count = frames + 1
    started = pl.pallas_call(
        inner_kernel,
        out_shape=jax.ShapeDtypeStruct((count, rows, columns, width), bf16),
        in_specs=[ANY] * 4 + [VMEM] * 3,
        out_specs=VMEM,
        scratch_shapes=[
            pltpu.VMEM((frames + taps, rows, columns, width), bf16),
            pltpu.VMEM((taps, rows, columns, width), bf16),
            pltpu.SemaphoreType.DMA((5,)),
        ],
        compiler_params=params(),
        cost_estimate=pl.CostEstimate(flops=3_000_000_000, bytes_accessed=4_000_000, transcendentals=0),
        name="inner",
    )(video, beyond, passed, passed_other, packed, line(first_bias), line(bias_other))
    portion = second_bias.shape[0]
    latents, given = pl.pallas_call(
        outer_kernel,
        out_shape=[
            jax.ShapeDtypeStruct((frames // 2, rows, columns, portion), bf16),
            jax.ShapeDtypeStruct((frames // 2, half, columns, portion), bf16),
        ],
        in_specs=[ANY] * 5 + [VMEM] * 6,
        out_specs=[VMEM] * 2,
        scratch_shapes=[
            pltpu.VMEM((count, rows, columns, width), bf16),
            pltpu.VMEM((frames + taps - 1, rows, columns, width), bf16),
            pltpu.SemaphoreType.DMA((5,)),
        ],
        compiler_params=params(),
        cost_estimate=pl.CostEstimate(flops=3_000_000_000, bytes_accessed=4_000_000, transcendentals=0),
        name="outer",
    )(
        own, beyond, passed, passed_beyond, started, packed, second_weight,
        line(first_bias), line(bias_other), line(second_bias), line(out_other),
    )
    taken = cycle(given, "chan")
    return lax.dynamic_update_slice_in_dim(latents, taken, (1 - core) * half, 1)


def solution(mesh):
    placed = (
        P(("clip", "slab"), "tile", None, None),
        P(None, None, None, None, "chan"),
        P("chan"),
        P(),
        P("chan"),
    )
    return jax.shard_map(
        shards,
        mesh=mesh,
        in_specs=placed,
        out_specs=P(("clip", "slab"), "tile", None, "chan"),
        check_vma=False,
    )
```

```python
import jax
import jax.numpy as jnp
from jax import lax
from jax.experimental import pallas as pl
from jax.experimental.pallas import tpu as pltpu
from jax.sharding import PartitionSpec as P

VMEM = pl.BlockSpec(memory_space=pltpu.VMEM)
ANY = pl.BlockSpec(memory_space=pl.ANY)
HBM = pl.BlockSpec(memory_space=pltpu.HBM)
LIMIT = 20 * 1024 * 1024
TAIL = 16


def silu(value):
    return value / (1.0 + jnp.exp(-value))


def shifted_sum(parts, columns):
    size = parts[0].shape[0]
    cell = lax.broadcasted_iota(jnp.int32, parts[0].shape, 0) % columns
    low = jnp.where(cell == 0, 0.0, pltpu.roll(parts[0], 1, 0))
    high = jnp.where(cell == columns - 1, 0.0, pltpu.roll(parts[2], size - 1, 0))
    return parts[1] + low + high


def border_known():
    core, tile = lax.axis_index("chan"), lax.axis_index("tile")
    last = lax.axis_size("tile") - 1
    return jnp.logical_not(jnp.logical_or((core == 0) & (tile == 0), (core == 1) & (tile == last)))


def thirds(value):
    high = value.astype(jnp.bfloat16)
    left = value - high.astype(jnp.float32)
    middle = left.astype(jnp.bfloat16)
    return [high, middle, (left - middle.astype(jnp.float32)).astype(jnp.bfloat16)]


def stage_kernel(video, weight, first_bias, second_bias, own, rest, staged, first_line, second_line, sems):
    core = lax.axis_index("chan")
    half = own.shape[1]
    size = weight.shape[0]
    pairs = (
        (video.at[:, pl.ds(core * half, half)], own),
        (video.at[:, pl.ds((1 - core) * half, half)], rest),
        (weight, staged.at[0:size]),
        (first_bias, first_line),
        (second_bias, second_line),
    )
    copies = [pltpu.make_async_copy(source, target, sems.at[k]) for k, (source, target) in enumerate(pairs)]
    for copy in copies:
        copy.start()
    for copy in copies[3:]:
        copy.wait()
    width = staged.shape[1]
    first = first_line[...]
    first = jnp.concatenate([first, jnp.zeros((1, width - first.shape[1]), first.dtype)], axis=1)
    rows = thirds(first) + thirds(second_line[...])
    rows.append(jnp.zeros((TAIL - len(rows), width), jnp.bfloat16))
    staged[size:] = jnp.concatenate(rows, axis=0)
    for copy in copies[:3]:
        copy.wait()


def join_kernel(kept, taken, latents, sems):
    core = lax.axis_index("chan")
    half = kept.shape[1]
    copies = [
        pltpu.make_async_copy(part, latents.at[:, pl.ds(place * half, half)], sems.at[k])
        for k, (part, place) in enumerate(((kept, core), (taken, 1 - core)))
    ]
    for copy in copies:
        copy.start()
    for copy in copies:
        copy.wait()


def pack_kernel(own, other, inner, outer, bias_first, bias_second):
    core = lax.axis_index("chan")
    known = border_known()
    taps = 3
    rows = taps + 1
    width = own.shape[1]
    size = own.shape[0] - TAIL
    channels = size // taps**3

    def lines(source):
        last = source[size:].astype(jnp.float32)
        added = [last[3 * k : 3 * k + 1] + last[3 * k + 1 : 3 * k + 2] + last[3 * k + 2 : 3 * k + 3] for k in range(2)]
        return added[0][:, :channels], added[1]

    mine, theirs = lines(own), lines(other)
    low = [jnp.where(core == 0, m, t) for m, t in zip(mine, theirs)]
    high = [jnp.where(core == 0, t, m) for m, t in zip(mine, theirs)]
    once = jnp.concatenate([low[0], high[0]], axis=1)
    bias_first[...] = jnp.concatenate([once, once], axis=1)
    bias_second[...] = jnp.concatenate([low[1], high[1]], axis=1)
    for a in range(taps):
        for e in range(taps):
            full = []
            for b in range(taps):
                at = ((a * taps + b) * taps + e) * channels
                mine, theirs = own[at : at + channels], other[at : at + channels]
                low = jnp.where(core == 0, mine, theirs)
                high = jnp.where(core == 0, theirs, mine)
                full.append(jnp.concatenate([low, high], axis=0).T)
            nothing = jnp.zeros_like(full[0])
            across = slice(e * 2 * width, (e + 1) * 2 * width)
            for i in range(rows):
                pair = [full[i - j] if 0 <= i - j < taps else nothing for j in range(2)]
                pair = jnp.concatenate(pair, axis=1)
                upper = i < rows // 2
                at = lax.rem(i + 2 * core, rows) + a * rows
                inner[pl.ds(pl.multiple_of(at * width, width), width), across] = pair
                at = lax.rem(i + 2 * (1 - core), rows) + a * rows
                used = known | (core == (1 if upper else 0))
                outer[pl.ds(pl.multiple_of(at * width, width), width), across] = jnp.where(
                    used, pair, jnp.zeros_like(pair)
                )


def first_layer(tile, frames, packed, bias):
    taps = 3
    rows = taps + 1
    left = jnp.concatenate(
        [
            jnp.concatenate([tile(f + a, k) for f in frames], axis=0)
            for a in range(taps)
            for k in range(rows)
        ],
        axis=1,
    )
    double = packed.shape[1] // taps
    columns = left.shape[0] // len(frames)
    parts = [
        jnp.dot(left, packed[:, e * double : (e + 1) * double], preferred_element_type=jnp.float32)
        for e in range(taps)
    ]
    return silu(shifted_sum(parts, columns) + bias).astype(jnp.bfloat16)


def second_layer(hidden, place, late, second):
    taps = second.shape[0]
    columns, width = hidden.shape[2:]
    results = (hidden.shape[0] - 1) // 2

    def added(rows):
        left = jnp.concatenate(
            [
                jnp.concatenate([hidden[2 * t + a, place + j] for t in range(results)], axis=0)
                for a in range(taps)
                for j, _ in rows
            ],
            axis=1,
        )
        parts = [
            jnp.dot(
                left,
                jnp.concatenate([second[a, b, e] for a in range(taps) for _, b in rows], axis=0),
                preferred_element_type=jnp.float32,
            )
            for e in range(taps)
        ]
        return shifted_sum(parts, columns)

    return added([(0, 1 - late), (1, 2 - late)]), added([(late, 2 * (1 - late))])


def inner_kernel(own, rest, beyond, passed, passed_other, packed, packed_outer, bias, second, hidden, partial):
    core = lax.axis_index("chan")
    slab = lax.axis_index("slab")
    known = border_known()
    frames, half, columns, width = own.shape
    mine, over = half * (1 - core), half * core

    def tile(f, k):
        if f >= frames:
            return own[f - frames, k] if k < half else rest[f - frames, k - half]
        row = passed[f, k] if k < half else passed_other[f, k - half]
        return jnp.where(slab > 0, row, jnp.zeros_like(row))

    count = hidden.shape[0]
    result = first_layer(tile, range(count), packed, bias[...])
    for n in range(count):
        for j in range(2):
            row = result[n * columns : (n + 1) * columns, j * width : (j + 1) * width]
            if n < 2:
                row = jnp.where(slab > 0, row, jnp.zeros_like(row))
            hidden[n, mine + j] = row

    def edge(f, k):
        return own[f - frames, k] if k < half else beyond[f - frames, k - half]

    result = first_layer(edge, [count - 1], packed_outer, bias[...])
    for j in range(2):
        row = result[:, j * width : (j + 1) * width]
        hidden[count - 1, over + j] = jnp.where(known | (core != j), row, jnp.zeros_like(row))
    both, one = second_layer(hidden, mine, core, second)
    partial[1 - core] = both
    partial[core] = one


def outer_kernel(
    own, beyond, passed, passed_beyond, started, partial, packed, second, bias, bias_second, kept, given, hidden
):
    core = lax.axis_index("chan")
    slab = lax.axis_index("slab")
    known = border_known()
    frames, half, columns, width = own.shape
    mine, over = half * (1 - core), half * core
    count = hidden.shape[0]
    def tile(f, k):
        if f >= frames:
            return own[f - frames, k] if k < half else beyond[f - frames, k - half]
        row = passed[f, k] if k < half else passed_beyond[f, k - half]
        return jnp.where(slab > 0, row, jnp.zeros_like(row))

    result = first_layer(tile, range(count - 1), packed, bias[...])
    for n in range(count - 1):
        for j in range(2):
            row = result[n * columns : (n + 1) * columns, j * width : (j + 1) * width]
            inside = known | (core != j)
            if n < 2:
                inside = inside & (slab > 0)
            hidden[n, over + j] = jnp.where(inside, row, jnp.zeros_like(row))
    for j in range(half):
        hidden[count - 1, over + j] = started[count - 1, over + j]
    portion = given.shape[3]
    results = given.shape[0]
    for row, value in zip((core, 1 - core), second_layer(hidden, over, 1 - core, second)):
        total = silu(value + partial[row] + bias_second[...]).astype(jnp.bfloat16)
        total = total.reshape(results, columns, 2 * portion)
        low, high = total[..., :portion], total[..., portion:]
        kept[:, row] = jnp.where(core == 0, low, high)
        given[:, row] = jnp.where(core == 0, high, low)


def cycle(value, axis):
    count = lax.axis_size(axis)
    return lax.ppermute(value, axis, [(i, (i + 1) % count) for i in range(count)])


def across_border(value):
    clips, tiles = lax.axis_size("clip"), lax.axis_size("tile")
    pairs = []
    for clip in range(clips):
        at = lambda c, t, k: (c * tiles + t) * 2 + k
        for tile in range(tiles - 1):
            pairs.append((at(clip, tile, 1), at(clip, tile + 1, 0)))
            pairs.append((at(clip, tile + 1, 0), at(clip, tile, 1)))
        if clips > 1:
            pairs.append((at(clip, 0, 0), at((clip + 1) % clips, 0, 0)))
            pairs.append((at(clip, tiles - 1, 1), at((clip + 1) % clips, tiles - 1, 1)))
    return lax.ppermute(value, ("clip", "tile", "chan"), pairs)


def shards(video, first_weight, first_bias, second_weight, second_bias):
    frames, rows, columns, width = video.shape
    half = rows // 2
    taps = first_weight.shape[0]
    assert half == taps - 1 and frames == 2 * (taps - 1) and lax.axis_size("chan") == 2
    bf16 = jnp.bfloat16
    shape = jax.ShapeDtypeStruct
    small = pl.CostEstimate(flops=1000, bytes_accessed=1000, transcendentals=0)

    def call(kernel, outs, ins, scratch, *operands, out_specs=None, limit=LIMIT):
        return pl.pallas_call(
            kernel,
            out_shape=outs,
            in_specs=ins,
            out_specs=[VMEM] * len(outs) if out_specs is None else out_specs,
            scratch_shapes=scratch,
            compiler_params=pltpu.CompilerParams(vmem_limit_bytes=limit),
            cost_estimate=small,
        )(*operands)

    tall = shape((frames, half, columns, width), bf16)
    turned = jnp.swapaxes(first_weight, 3, 4).reshape(-1, width)
    near = lambda value: pltpu.with_memory_space_constraint(value, pltpu.HBM)
    own, rest, staged = call(
        stage_kernel,
        [
            pltpu.VMEM(tall.shape, bf16),
            pltpu.VMEM(tall.shape, bf16),
            pltpu.VMEM((turned.shape[0] + TAIL, width), bf16),
        ],
        [HBM] * 4,
        [
            pltpu.VMEM((1, first_bias.shape[0]), jnp.float32),
            pltpu.VMEM((1, second_bias.shape[0]), jnp.float32),
            pltpu.SemaphoreType.DMA((5,)),
        ],
        near(video), near(turned), near(first_bias.reshape(1, -1)), near(second_bias.reshape(1, -1)),
    )
    passed = cycle(own, "slab")
    beyond = across_border(own)
    staged_other = cycle(staged, "chan")
    matrix = shape((taps * (taps + 1) * width, taps * 2 * width), bf16)
    packed, packed_outer, bias_first, bias_last = call(
        pack_kernel,
        [matrix, matrix, shape((1, 2 * width), jnp.float32), shape((1, second_weight.shape[4]), jnp.float32)],
        [VMEM] * 2,
        [],
        staged, staged_other,
    )
    passed_beyond = across_border(passed)
    passed_other = cycle(passed, "chan")
    count = frames + 1
    started, partial = call(
        inner_kernel,
        [
            shape((count, rows, columns, width), bf16),
            shape((half, frames // 2 * columns, second_weight.shape[4]), jnp.float32),
        ],
        [VMEM] * 9,
        [],
        own, rest, beyond, passed, passed_other, packed, packed_outer, bias_first, second_weight,
    )
    part = shape((frames // 2, half, columns, second_bias.shape[0]), bf16)
    kept, given = call(
        outer_kernel,
        [part, part],
        [VMEM] * 10,
        [pltpu.VMEM((count, rows, columns, width), bf16)],
        own, beyond, passed, passed_beyond, started, partial, packed_outer, second_weight, bias_first, bias_last,
    )
    taken = cycle(given, "chan")
    (latents,) = call(
        join_kernel,
        [shape((frames // 2, rows, columns, second_bias.shape[0]), bf16)],
        [VMEM] * 2,
        [pltpu.SemaphoreType.DMA((2,))],
        kept, taken,
        out_specs=[ANY],
    )
    return latents


def solution(mesh):
    placed = (
        P(("clip", "slab"), "tile", None, None),
        P(None, None, None, None, "chan"),
        P("chan"),
        P(),
        P("chan"),
    )
    return jax.shard_map(
        shards,
        mesh=mesh,
        in_specs=placed,
        out_specs=P(("clip", "slab"), "tile", None, "chan"),
        check_vma=False,
    )
```

```python
import functools

import jax
import jax.numpy as jnp
from jax import lax
from jax.experimental import pallas as pl
from jax.experimental.pallas import tpu as pltpu
from jax.sharding import PartitionSpec as P

VMEM = pl.BlockSpec(memory_space=pltpu.VMEM)
ANY = pl.BlockSpec(memory_space=pl.ANY)
HBM = pl.BlockSpec(memory_space=pltpu.HBM)
LIMIT = 20 * 1024 * 1024
TAIL = 16


def silu(value):
    half = 0.5 * value
    return half + half * jnp.tanh(half)


def shifted_sum(parts, columns):
    size, width = parts[0].shape
    before, here, after = (part.reshape(size // columns, columns, width) for part in parts)
    cell = lax.broadcasted_iota(jnp.int32, (1, columns, width), 1)
    before = jnp.where(cell == 0, 0.0, pltpu.roll(before, 1, 1))
    after = jnp.where(cell == columns - 1, 0.0, pltpu.roll(after, columns - 1, 1))
    return (here + before + after).reshape(size, width)


def border_known():
    core, tile = lax.axis_index("chan"), lax.axis_index("tile")
    last = lax.axis_size("tile") - 1
    return jnp.logical_not(jnp.logical_or((core == 0) & (tile == 0), (core == 1) & (tile == last)))


def thirds(value):
    high = value.astype(jnp.bfloat16)
    left = value - high.astype(jnp.float32)
    middle = left.astype(jnp.bfloat16)
    return [high, middle, (left - middle.astype(jnp.float32)).astype(jnp.bfloat16)]


def stage_kernel(video, weight, first_bias, second_bias, own, late, rest, staged, first_line, second_line, sems):
    core = lax.axis_index("chan")
    half = own.shape[1]
    size = weight.shape[0]
    pairs = (
        (video.at[:, pl.ds(core * half, half)], own),
        (video.at[video.shape[0] - late.shape[0] :, pl.ds(core * half, half)], late),
        (video.at[:, pl.ds((1 - core) * half, half)], rest),
        (weight, staged.at[0:size]),
        (first_bias, first_line),
        (second_bias, second_line),
    )
    copies = [pltpu.make_async_copy(source, target, sems.at[k]) for k, (source, target) in enumerate(pairs)]
    for copy in copies:
        copy.start()
    for copy in copies[4:]:
        copy.wait()
    width = staged.shape[1]
    first = first_line[...]
    first = jnp.concatenate([first, jnp.zeros((1, width - first.shape[1]), first.dtype)], axis=1)
    rows = thirds(first) + thirds(second_line[...])
    rows.append(jnp.zeros((TAIL - len(rows), width), jnp.bfloat16))
    staged[size:] = jnp.concatenate(rows, axis=0)
    for copy in copies[:4]:
        copy.wait()


def join_kernel(*refs):
    frames = len(refs) // 2 - 1
    latents, sems = refs[2 * frames :]
    core = lax.axis_index("chan")
    half = refs[0].shape[0]
    copies = []
    for t in range(frames):
        for k, place in enumerate((core, 1 - core)):
            target = latents.at[t, pl.ds(place * half, half)]
            copies.append(pltpu.make_async_copy(refs[2 * t + k], target, sems.at[2 * t + k]))
    for copy in copies:
        copy.start()
    for copy in copies:
        copy.wait()


def pack_kernel(own, other, inner, outer, bias_first, bias_second):
    core = lax.axis_index("chan")
    known = border_known()
    taps = 3
    rows = taps + 1
    width = own.shape[1]
    size = own.shape[0] - TAIL
    channels = size // taps**3

    def lines(source):
        last = source[size:].astype(jnp.float32)
        added = [last[3 * k : 3 * k + 1] + last[3 * k + 1 : 3 * k + 2] + last[3 * k + 2 : 3 * k + 3] for k in range(2)]
        return added[0][:, :channels], added[1]

    mine, theirs = lines(own), lines(other)
    low = [jnp.where(core == 0, m, t) for m, t in zip(mine, theirs)]
    high = [jnp.where(core == 0, t, m) for m, t in zip(mine, theirs)]
    once = jnp.concatenate([low[0], high[0]], axis=1)
    bias_first[...] = jnp.concatenate([once, once], axis=1)
    bias_second[...] = jnp.concatenate([low[1], high[1]], axis=1)
    for a in range(taps):
        for e in range(taps):
            full = []
            for b in range(taps):
                at = ((a * taps + b) * taps + e) * channels
                mine, theirs = own[at : at + channels], other[at : at + channels]
                low = jnp.where(core == 0, mine, theirs)
                high = jnp.where(core == 0, theirs, mine)
                full.append(jnp.concatenate([low, high], axis=0).T)
            nothing = jnp.zeros_like(full[0])
            across = slice(e * 2 * width, (e + 1) * 2 * width)
            for i in range(rows):
                pair = [full[i - j] if 0 <= i - j < taps else nothing for j in range(2)]
                pair = jnp.concatenate(pair, axis=1)
                upper = i < rows // 2
                at = lax.rem(i + 2 * core, rows) + a * rows
                inner[pl.ds(pl.multiple_of(at * width, width), width), across] = pair
                at = lax.rem(i + 2 * (1 - core), rows) + a * rows
                used = known | (core == (1 if upper else 0))
                outer[pl.ds(pl.multiple_of(at * width, width), width), across] = jnp.where(
                    used, pair, jnp.zeros_like(pair)
                )


def first_layer(tile, frames, packed, bias):
    taps = 3
    rows = taps + 1
    left = jnp.concatenate(
        [
            jnp.concatenate([tile(f + a, k) for f in frames], axis=0)
            for a in range(taps)
            for k in range(rows)
        ],
        axis=1,
    )
    double = packed.shape[1] // taps
    columns = left.shape[0] // len(frames)
    parts = [
        jnp.dot(left, packed[:, e * double : (e + 1) * double], preferred_element_type=jnp.float32)
        for e in range(taps)
    ]
    return silu(shifted_sum(parts, columns) + bias).astype(jnp.bfloat16)


def second_layer(tile, frames, late, second):
    def added(rows):
        left = jnp.concatenate(
            [jnp.concatenate([tile(n, j) for n in frames[a]], axis=0) for a in frames for j, _ in rows], axis=1
        )
        parts = [
            jnp.dot(
                left,
                jnp.concatenate([second[a, b, e] for a in frames for _, b in rows], axis=0),
                preferred_element_type=jnp.float32,
            )
            for e in range(second.shape[2])
        ]
        return shifted_sum(parts, tile(frames[next(iter(frames))][0], 0).shape[0])

    return (1 - late, added([(0, 1 - late), (1, 2 - late)])), (late, added([(late, 2 * (1 - late))]))


def put_rows(result, target, start, columns, masks):
    width = target.shape[-1]
    for n in range(result.shape[0] // columns):
        for j in range(2):
            row = result[n * columns : (n + 1) * columns, j * width : (j + 1) * width]
            target[start + n, j] = row if masks is None else jnp.where(masks[j], row, jnp.zeros_like(row))


def border_masks():
    core, known = lax.axis_index("chan"), border_known()
    return [known | (core != j) for j in range(2)]


def ahead_kernel(own, beside, packed, bias, hidden, *, border):
    half, columns = own.shape[1:3]

    def tile(f, k):
        return own[f, k] if k < half else beside[f, k - half]

    result = first_layer(tile, range(hidden.shape[0]), packed, bias[...])
    put_rows(result, hidden, 0, columns, border_masks() if border else None)


def behind(own, beside, passed, passed_beside, packed, bias, hidden, start, masks):
    early, half, columns = passed.shape[:3]
    follows = lax.axis_index("slab") > 0

    def tile(f, k):
        if f >= early:
            return own[f - early, k] if k < half else beside[f - early, k - half]
        row = passed[f, k] if k < half else passed_beside[f, k - half]
        return jnp.where(follows, row, jnp.zeros_like(row))

    put_rows(first_layer(tile, range(early), packed, bias[...]), hidden, start, columns, masks)


def inner_kernel(own, rest, passed, passed_other, packed, bias, ahead, second, partial, hidden):
    early, _, columns = passed.shape[:3]
    behind(own, rest, passed, passed_other, packed, bias, hidden, 0, None)
    hidden[early] = ahead[0]
    add_layers(hidden, lax.axis_index("chan"), second, partial, None)


def add_layers(hidden, late, second, target, base):
    columns = hidden.shape[2]
    tile = lambda n, j: hidden[n, j]
    ends = second_layer(tile, {2: [0, 2]}, late, second)
    starts = second_layer(tile, {0: [0], 1: [1]}, late, second)
    for (row, end), (_, start) in zip(ends, starts):
        first, later = end[:columns], end[columns:] + start
        if base is not None:
            first, later = first + base[row, :columns], later + base[row, columns:]
        target[row, :columns] = first
        target[row, columns:] = later


def from_earlier(handed):
    follows = lax.axis_index("slab") > 0

    def tile(n, j):
        row = handed[n, j]
        return jnp.where(follows, row, jnp.zeros_like(row))

    return tile


def finish(value, bias, row, kept, given):
    core = lax.axis_index("chan")
    total = silu(value + bias[...]).astype(jnp.bfloat16)
    portion = kept.shape[-1]
    low, high = total[:, :portion], total[:, portion:]
    kept[row] = jnp.where(core == 0, low, high)
    given[row] = jnp.where(core == 0, high, low)


def outer_kernel(
    handed, own, beyond, passed, packed, bias, ahead, second, bias_second, partial, passed_beyond,
    kept, given, left, hidden, total,
):
    core = lax.axis_index("chan")
    early, _, columns = passed.shape[:3]
    behind(own, beyond, passed, passed_beyond, packed, bias, hidden, 0, border_masks())
    hidden[early] = ahead[0]
    add_layers(hidden, 1 - core, second, total, partial)
    for row, value in second_layer(from_earlier(handed), {0: [0], 1: [1]}, core, second):
        left[row] = total[row, :columns] + value
    for row in range(total.shape[0]):
        finish(total[row, columns:], bias_second, row, kept, given)


def last_kernel(handed, second, bias_second, left, kept, given):
    for row, value in second_layer(from_earlier(handed), {0: [0], 1: [1]}, 1 - lax.axis_index("chan"), second):
        finish(left[row] + value, bias_second, row, kept, given)


def cycle(value, axis):
    count = lax.axis_size(axis)
    return lax.ppermute(value, axis, [(i, (i + 1) % count) for i in range(count)])


def across_border(value):
    clips, tiles = lax.axis_size("clip"), lax.axis_size("tile")
    pairs = []
    for clip in range(clips):
        at = lambda c, t, k: (c * tiles + t) * 2 + k
        for tile in range(tiles - 1):
            pairs.append((at(clip, tile, 1), at(clip, tile + 1, 0)))
            pairs.append((at(clip, tile + 1, 0), at(clip, tile, 1)))
        if clips > 1:
            pairs.append((at(clip, 0, 0), at((clip + 1) % clips, 0, 0)))
            pairs.append((at(clip, tiles - 1, 1), at((clip + 1) % clips, tiles - 1, 1)))
    return lax.ppermute(value, ("clip", "tile", "chan"), pairs)


def shards(video, first_weight, first_bias, second_weight, second_bias):
    frames, rows, columns, width = video.shape
    half = rows // 2
    taps = first_weight.shape[0]
    assert half == taps - 1 and frames == 2 * (taps - 1) and lax.axis_size("chan") == 2
    bf16 = jnp.bfloat16
    shape = jax.ShapeDtypeStruct
    small = pl.CostEstimate(flops=1000, bytes_accessed=1000, transcendentals=0)

    def call(kernel, outs, ins, scratch, *operands, out_specs=None, limit=LIMIT):
        return pl.pallas_call(
            kernel,
            out_shape=outs,
            in_specs=ins,
            out_specs=[VMEM] * len(outs) if out_specs is None else out_specs,
            scratch_shapes=scratch,
            compiler_params=pltpu.CompilerParams(vmem_limit_bytes=limit),
            cost_estimate=small,
        )(*operands)

    early = frames // 2
    tall, short = (shape((count, half, columns, width), bf16) for count in (frames, early))
    turned = jnp.swapaxes(first_weight, 3, 4).reshape(-1, width)
    far = lambda value: pltpu.with_memory_space_constraint(value, pltpu.HBM)
    own, late, rest, staged = call(
        stage_kernel,
        [
            pltpu.VMEM(tall.shape, bf16),
            pltpu.VMEM(short.shape, bf16),
            pltpu.VMEM(tall.shape, bf16),
            pltpu.VMEM((turned.shape[0] + TAIL, width), bf16),
        ],
        [HBM] * 4,
        [
            pltpu.VMEM((1, first_bias.shape[0]), jnp.float32),
            pltpu.VMEM((1, second_bias.shape[0]), jnp.float32),
            pltpu.SemaphoreType.DMA((6,)),
        ],
        far(video), far(turned), far(first_bias.reshape(1, -1)), far(second_bias.reshape(1, -1)),
    )
    beyond = across_border(own)
    passed = cycle(late, "slab")
    staged_other = cycle(staged, "chan")
    matrix = shape((taps * (taps + 1) * width, taps * 2 * width), bf16)
    channels = second_weight.shape[4]
    packed, packed_outer, bias_first, bias_last = call(
        pack_kernel,
        [matrix, matrix, shape((1, 2 * width), jnp.float32), shape((1, channels), jnp.float32)],
        [VMEM] * 2,
        [],
        staged, staged_other,
    )
    (ahead_inner,) = call(
        functools.partial(ahead_kernel, border=False), [short], [VMEM] * 4, [], own, rest, packed, bias_first
    )
    handed_inner = cycle(ahead_inner, "slab")
    passed, _ = lax.optimization_barrier((passed, ahead_inner))
    passed_beyond = across_border(passed)
    passed_other = cycle(passed, "chan")
    beyond, passed_other = lax.optimization_barrier((beyond, passed_other))
    (ahead_outer,) = call(
        functools.partial(ahead_kernel, border=True), [short], [VMEM] * 4, [], own, beyond, packed_outer, bias_first
    )
    handed_outer = cycle(ahead_outer, "slab")
    (partial,) = call(
        inner_kernel,
        [shape((half, early * columns, channels), jnp.float32)],
        [VMEM] * 8,
        [pltpu.VMEM((early + 1, half, columns, width), bf16)],
        own, rest, passed, passed_other, packed, bias_first, ahead_inner, second_weight,
    )
    part = shape((half, columns, second_bias.shape[0]), bf16)
    handed_inner, partial = lax.optimization_barrier((handed_inner, partial))
    kept_second, given_second, left = call(
        outer_kernel,
        [part, part, shape((half, columns, channels), jnp.float32)],
        [VMEM] * 11,
        [
            pltpu.VMEM((early + 1, half, columns, width), bf16),
            pltpu.VMEM((half, early * columns, channels), jnp.float32),
        ],
        handed_inner, own, beyond, passed, packed_outer, bias_first, ahead_outer, second_weight,
        bias_last, partial, passed_beyond,
    )
    taken_second = cycle(given_second, "chan")
    kept_first, given_first = call(
        last_kernel, [part, part], [VMEM] * 4, [], handed_outer, second_weight, bias_last, left
    )
    taken_first = cycle(given_first, "chan")
    (latents,) = call(
        join_kernel,
        [shape((early, rows, columns, second_bias.shape[0]), bf16)],
        [VMEM] * 4,
        [pltpu.SemaphoreType.DMA((4,))],
        kept_first, taken_first, kept_second, taken_second,
        out_specs=[ANY],
    )
    return latents


def solution(mesh):
    placed = (
        P(("clip", "slab"), "tile", None, None),
        P(None, None, None, None, "chan"),
        P("chan"),
        P(),
        P("chan"),
    )
    return jax.shard_map(
        shards,
        mesh=mesh,
        in_specs=placed,
        out_specs=P(("clip", "slab"), "tile", None, "chan"),
        check_vma=False,
    )
```

```python
import functools

import jax
import jax.numpy as jnp
from jax import lax
from jax.experimental import pallas as pl
from jax.experimental.pallas import tpu as pltpu
from jax.sharding import PartitionSpec as P

VMEM = pl.BlockSpec(memory_space=pltpu.VMEM)
ANY = pl.BlockSpec(memory_space=pl.ANY)
HBM = pl.BlockSpec(memory_space=pltpu.HBM)
LIMIT = 20 * 1024 * 1024
TAIL = 16


def silu(value):
    half = 0.5 * value
    return half + half * jnp.tanh(half)


def shifted_sum(parts, columns):
    size, width = parts[0].shape
    before, here, after = (part.reshape(size // columns, columns, width) for part in parts)
    cell = lax.broadcasted_iota(jnp.int32, (1, columns, width), 1)
    before = jnp.where(cell == 0, 0.0, pltpu.roll(before, 1, 1))
    after = jnp.where(cell == columns - 1, 0.0, pltpu.roll(after, columns - 1, 1))
    return (here + before + after).reshape(size, width)


def border_known():
    core, tile = lax.axis_index("chan"), lax.axis_index("tile")
    last = lax.axis_size("tile") - 1
    return jnp.logical_not(jnp.logical_or((core == 0) & (tile == 0), (core == 1) & (tile == last)))


def thirds(value):
    high = value.astype(jnp.bfloat16)
    left = value - high.astype(jnp.float32)
    middle = left.astype(jnp.bfloat16)
    return [high, middle, (left - middle.astype(jnp.float32)).astype(jnp.bfloat16)]


def stage_kernel(video, weight, first_bias, second_bias, front, late, rest_front, rest_late, staged, first_line, second_line, sems):
    core = lax.axis_index("chan")
    early, half = front.shape[:2]
    size = weight.shape[0]
    pairs = (
        (video.at[:early, pl.ds(core * half, half)], front),
        (video.at[early:, pl.ds(core * half, half)], late),
        (video.at[:early, pl.ds((1 - core) * half, half)], rest_front),
        (video.at[early:, pl.ds((1 - core) * half, half)], rest_late),
        (weight, staged.at[0:size]),
        (first_bias, first_line),
        (second_bias, second_line),
    )
    copies = [pltpu.make_async_copy(source, target, sems.at[k]) for k, (source, target) in enumerate(pairs)]
    for copy in copies:
        copy.start()
    for copy in copies[5:]:
        copy.wait()
    width = staged.shape[1]
    first = first_line[...]
    first = jnp.concatenate([first, jnp.zeros((1, width - first.shape[1]), first.dtype)], axis=1)
    rows = thirds(first) + thirds(second_line[...])
    rows.append(jnp.zeros((TAIL - len(rows), width), jnp.bfloat16))
    staged[size:] = jnp.concatenate(rows, axis=0)
    for copy in copies[:5]:
        copy.wait()


def join_kernel(*refs):
    frames = len(refs) // 2 - 1
    latents, sems = refs[2 * frames :]
    core = lax.axis_index("chan")
    half = refs[0].shape[0]
    copies = []
    for t in range(frames):
        for k, place in enumerate((core, 1 - core)):
            target = latents.at[t, pl.ds(place * half, half)]
            copies.append(pltpu.make_async_copy(refs[2 * t + k], target, sems.at[2 * t + k]))
    for copy in copies:
        copy.start()
    for copy in copies:
        copy.wait()


def pack_kernel(own, other, inner, outer, bias_first, bias_second):
    core = lax.axis_index("chan")
    known = border_known()
    taps = 3
    rows = taps + 1
    width = own.shape[1]
    size = own.shape[0] - TAIL
    channels = size // taps**3

    def lines(source):
        last = source[size:].astype(jnp.float32)
        added = [last[3 * k : 3 * k + 1] + last[3 * k + 1 : 3 * k + 2] + last[3 * k + 2 : 3 * k + 3] for k in range(2)]
        return added[0][:, :channels], added[1]

    mine, theirs = lines(own), lines(other)
    low = [jnp.where(core == 0, m, t) for m, t in zip(mine, theirs)]
    high = [jnp.where(core == 0, t, m) for m, t in zip(mine, theirs)]
    once = jnp.concatenate([low[0], high[0]], axis=1)
    bias_first[...] = jnp.concatenate([once, once], axis=1)
    bias_second[...] = jnp.concatenate([low[1], high[1]], axis=1)
    for a in range(taps):
        for e in range(taps):
            full = []
            for b in range(taps):
                at = ((a * taps + b) * taps + e) * channels
                mine, theirs = own[at : at + channels], other[at : at + channels]
                low = jnp.where(core == 0, mine, theirs)
                high = jnp.where(core == 0, theirs, mine)
                full.append(jnp.concatenate([low, high], axis=0).T)
            nothing = jnp.zeros_like(full[0])
            across = slice(e * 2 * width, (e + 1) * 2 * width)
            for i in range(rows):
                pair = [full[i - j] if 0 <= i - j < taps else nothing for j in range(2)]
                pair = jnp.concatenate(pair, axis=1)
                upper = i < rows // 2
                at = lax.rem(i + 2 * core, rows) + a * rows
                inner[pl.ds(pl.multiple_of(at * width, width), width), across] = pair
                at = lax.rem(i + 2 * (1 - core), rows) + a * rows
                used = known | (core == (1 if upper else 0))
                outer[pl.ds(pl.multiple_of(at * width, width), width), across] = jnp.where(
                    used, pair, jnp.zeros_like(pair)
                )


def first_layer(tile, frames, packed, bias):
    taps = 3
    rows = taps + 1
    left = jnp.concatenate(
        [
            jnp.concatenate([tile(f + a, k) for f in frames], axis=0)
            for a in range(taps)
            for k in range(rows)
        ],
        axis=1,
    )
    double = packed.shape[1] // taps
    columns = left.shape[0] // len(frames)
    parts = [
        jnp.dot(left, packed[:, e * double : (e + 1) * double], preferred_element_type=jnp.float32)
        for e in range(taps)
    ]
    return silu(shifted_sum(parts, columns) + bias).astype(jnp.bfloat16)


def second_layer(terms, second):
    left = jnp.concatenate([tile for tile, _, _ in terms], axis=1)
    parts = [
        jnp.dot(
            left,
            jnp.concatenate([second[a, b, e] for _, a, b in terms], axis=0),
            preferred_element_type=jnp.float32,
        )
        for e in range(second.shape[2])
    ]
    return shifted_sum(parts, left.shape[0])


def terms_of(tile, frames, late):
    both = [(tile(n, j), a, 1 - late + j) for n, a in frames for j in range(2)]
    return both, [(tile(n, late), a, 2 * (1 - late)) for n, a in frames]


def put_rows(result, target, start, columns, masks):
    width = target.shape[-1]
    for n in range(result.shape[0] // columns):
        for j in range(2):
            row = result[n * columns : (n + 1) * columns, j * width : (j + 1) * width]
            target[start + n, j] = row if masks is None else jnp.where(masks[j], row, jnp.zeros_like(row))


def border_masks():
    core, known = lax.axis_index("chan"), border_known()
    return [known | (core != j) for j in range(2)]


def ahead_kernel(front, late, *refs, border):
    *beside, packed, bias, hidden = refs
    half, columns = front.shape[1:3]

    def frame(parts, f):
        return (parts[0], f) if f < parts[0].shape[0] else frame(parts[1:], f - parts[0].shape[0])

    def tile(f, k):
        part, at = frame((front, late) if k < half else beside, f)
        return part[at, k % half]

    result = first_layer(tile, range(hidden.shape[0]), packed, bias[...])
    put_rows(result, hidden, 0, columns, border_masks() if border else None)


def behind(own, beside, passed, passed_beside, packed, bias, hidden, start, masks):
    early, half, columns = passed.shape[:3]
    follows = lax.axis_index("slab") > 0

    def tile(f, k):
        if f >= early:
            return own[f - early, k] if k < half else beside[f - early, k - half]
        row = passed[f, k] if k < half else passed_beside[f, k - half]
        return jnp.where(follows, row, jnp.zeros_like(row))

    put_rows(first_layer(tile, range(early), packed, bias[...]), hidden, start, columns, masks)


def inner_kernel(own, rest, passed, passed_other, packed, bias, ahead, second, partial, hidden):
    behind(own, rest, passed, passed_other, packed, bias, hidden, 0, None)
    hidden[passed.shape[0]] = ahead[0]

    def store(t, row, value):
        partial[t, row] = value

    add_layers(hidden, lax.axis_index("chan"), second, store)


def add_layers(hidden, late, second, store):
    tile = lambda n, j: hidden[n, j]
    for t, frames in enumerate(([(0, 2)], [(0, 0), (1, 1), (2, 2)])):
        for row, terms in zip((1 - late, late), terms_of(tile, frames, late)):
            store(t, row, second_layer(terms, second))


def from_earlier(handed):
    follows = lax.axis_index("slab") > 0

    def tile(n, j):
        row = handed[n, j]
        return jnp.where(follows, row, jnp.zeros_like(row))

    return tile


def finish(value, bias, row, kept, given):
    core = lax.axis_index("chan")
    total = silu(value + bias[...]).astype(jnp.bfloat16)
    portion = kept.shape[-1]
    low, high = total[:, :portion], total[:, portion:]
    kept[row] = jnp.where(core == 0, low, high)
    given[row] = jnp.where(core == 0, high, low)


def outer_kernel(
    own, beyond, passed, passed_beyond, packed, bias, ahead, second, bias_second, partial, kept, given, left, hidden
):
    behind(own, beyond, passed, passed_beyond, packed, bias, hidden, 0, border_masks())
    hidden[passed.shape[0]] = ahead[0]

    def store(t, row, value):
        if t == 0:
            left[row] = partial[t, row] + value
        else:
            finish(partial[t, row] + value, bias_second, row, kept, given)

    add_layers(hidden, 1 - lax.axis_index("chan"), second, store)


def last_kernel(handed_inner, handed_outer, second, bias_second, left, kept, given):
    core = lax.axis_index("chan")
    frames = [(0, 0), (1, 1)]
    inner_both, inner_one = terms_of(from_earlier(handed_inner), frames, core)
    outer_both, outer_one = terms_of(from_earlier(handed_outer), frames, 1 - core)
    for row, terms in ((1 - core, inner_both + outer_one), (core, outer_both + inner_one)):
        finish(left[row] + second_layer(terms, second), bias_second, row, kept, given)


def cycle(value, axis):
    count = lax.axis_size(axis)
    return lax.ppermute(value, axis, [(i, (i + 1) % count) for i in range(count)])


def across_border(value):
    clips, tiles = lax.axis_size("clip"), lax.axis_size("tile")
    pairs = []
    for clip in range(clips):
        at = lambda c, t, k: (c * tiles + t) * 2 + k
        for tile in range(tiles - 1):
            pairs.append((at(clip, tile, 1), at(clip, tile + 1, 0)))
            pairs.append((at(clip, tile + 1, 0), at(clip, tile, 1)))
        if clips > 1:
            pairs.append((at(clip, 0, 0), at((clip + 1) % clips, 0, 0)))
            pairs.append((at(clip, tiles - 1, 1), at((clip + 1) % clips, tiles - 1, 1)))
    return lax.ppermute(value, ("clip", "tile", "chan"), pairs)


def shards(video, first_weight, first_bias, second_weight, second_bias):
    frames, rows, columns, width = video.shape
    half = rows // 2
    taps = first_weight.shape[0]
    assert half == taps - 1 and frames == 2 * (taps - 1) and lax.axis_size("chan") == 2
    bf16 = jnp.bfloat16
    shape = jax.ShapeDtypeStruct
    small = pl.CostEstimate(flops=1000, bytes_accessed=1000, transcendentals=0)

    def call(kernel, outs, ins, scratch, *operands, out_specs=None, limit=LIMIT):
        return pl.pallas_call(
            kernel,
            out_shape=outs,
            in_specs=ins,
            out_specs=[VMEM] * len(outs) if out_specs is None else out_specs,
            scratch_shapes=scratch,
            compiler_params=pltpu.CompilerParams(vmem_limit_bytes=limit),
            cost_estimate=small,
        )(*operands)

    early = frames // 2
    short = shape((early, half, columns, width), bf16)
    turned = jnp.swapaxes(first_weight, 3, 4).reshape(-1, width)
    far = lambda value: pltpu.with_memory_space_constraint(value, pltpu.HBM)
    front, late, rest_front, rest_late, staged = call(
        stage_kernel,
        [
            pltpu.VMEM(short.shape, bf16),
            pltpu.VMEM(short.shape, bf16),
            pltpu.VMEM(short.shape, bf16),
            pltpu.VMEM(short.shape, bf16),
            pltpu.VMEM((turned.shape[0] + TAIL, width), bf16),
        ],
        [HBM] * 4,
        [
            pltpu.VMEM((1, first_bias.shape[0]), jnp.float32),
            pltpu.VMEM((1, second_bias.shape[0]), jnp.float32),
            pltpu.SemaphoreType.DMA((7,)),
        ],
        far(video), far(turned), far(first_bias.reshape(1, -1)), far(second_bias.reshape(1, -1)),
    )
    beyond_front, beyond_late = across_border(front), across_border(late)
    passed = cycle(late, "slab")
    passed_other = cycle(rest_late, "slab")
    staged_other = cycle(staged, "chan")
    matrix = shape((taps * (taps + 1) * width, taps * 2 * width), bf16)
    channels = second_weight.shape[4]
    packed, packed_outer, bias_first, bias_last = call(
        pack_kernel,
        [matrix, matrix, shape((1, 2 * width), jnp.float32), shape((1, channels), jnp.float32)],
        [VMEM] * 2,
        [],
        staged, staged_other,
    )
    (ahead_inner,) = call(
        functools.partial(ahead_kernel, border=False), [short], [VMEM] * 6, [], front, late, rest_front, rest_late,
        packed, bias_first
    )
    handed_inner = cycle(ahead_inner, "slab")
    passed, _ = lax.optimization_barrier((passed, ahead_inner))
    passed_beyond = across_border(passed)
    (ahead_outer,) = call(
        functools.partial(ahead_kernel, border=True),
        [short],
        [VMEM] * 6,
        [],
        front, late, beyond_front, beyond_late, packed_outer, bias_first,
    )
    handed_outer = cycle(ahead_outer, "slab")
    (partial,) = call(
        inner_kernel,
        [shape((early, half, columns, channels), jnp.float32)],
        [VMEM] * 8,
        [pltpu.VMEM((early + 1, half, columns, width), bf16)],
        front, rest_front, passed, passed_other, packed, bias_first, ahead_inner, second_weight,
    )
    part = shape((half, columns, second_bias.shape[0]), bf16)
    handed_inner, partial = lax.optimization_barrier((handed_inner, partial))
    kept_second, given_second, left = call(
        outer_kernel,
        [part, part, shape((half, columns, channels), jnp.float32)],
        [VMEM] * 10,
        [pltpu.VMEM((early + 1, half, columns, width), bf16)],
        front, beyond_front, passed, passed_beyond, packed_outer, bias_first, ahead_outer, second_weight, bias_last, partial,
    )
    taken_second = cycle(given_second, "chan")
    kept_first, given_first = call(
        last_kernel, [part, part], [VMEM] * 5, [], handed_inner, handed_outer, second_weight, bias_last, left
    )
    taken_first = cycle(given_first, "chan")
    (latents,) = call(
        join_kernel,
        [shape((early, rows, columns, second_bias.shape[0]), bf16)],
        [VMEM] * 4,
        [pltpu.SemaphoreType.DMA((4,))],
        kept_first, taken_first, kept_second, taken_second,
        out_specs=[ANY],
    )
    return latents


def solution(mesh):
    placed = (
        P(("clip", "slab"), "tile", None, None),
        P(None, None, None, None, "chan"),
        P("chan"),
        P(),
        P("chan"),
    )
    return jax.shard_map(
        shards,
        mesh=mesh,
        in_specs=placed,
        out_specs=P(("clip", "slab"), "tile", None, "chan"),
        check_vma=False,
    )
```

```python
import functools

import jax
import jax.numpy as jnp
from jax import lax
from jax.experimental import pallas as pl
from jax.experimental.pallas import tpu as pltpu
from jax.sharding import PartitionSpec as P

VMEM = pl.BlockSpec(memory_space=pltpu.VMEM)
ANY = pl.BlockSpec(memory_space=pl.ANY)
HBM = pl.BlockSpec(memory_space=pltpu.HBM)
LIMIT = 20 * 1024 * 1024
TAIL = 16


def silu(value):
    half = 0.5 * value
    return half + half * jnp.tanh(half)


def shifted_sum(parts, columns):
    size, width = parts[0].shape
    before, here, after = (part.reshape(size // columns, columns, width) for part in parts)
    cell = lax.broadcasted_iota(jnp.int32, (1, columns, width), 1)
    before = jnp.where(cell == 0, 0.0, pltpu.roll(before, 1, 1))
    after = jnp.where(cell == columns - 1, 0.0, pltpu.roll(after, columns - 1, 1))
    return (here + before + after).reshape(size, width)


def lower_half():
    return lax.rem(lax.axis_index("chan") + lax.axis_index("tile"), 2)


def border_known():
    lower, tile = lower_half(), lax.axis_index("tile")
    last = lax.axis_size("tile") - 1
    return jnp.logical_not(jnp.logical_or((lower == 0) & (tile == 0), (lower == 1) & (tile == last)))


def thirds(value):
    high = value.astype(jnp.bfloat16)
    left = value - high.astype(jnp.float32)
    middle = left.astype(jnp.bfloat16)
    return [high, middle, (left - middle.astype(jnp.float32)).astype(jnp.bfloat16)]


def stage_kernel(video, weight, first_bias, second_bias, front, late, rest_front, rest_late, staged, first_line, second_line, sems):
    lower = lower_half()
    early, half = front.shape[:2]
    size = weight.shape[0]
    pairs = (
        (video.at[:early, pl.ds(lower * half, half)], front),
        (video.at[early:, pl.ds(lower * half, half)], late),
        (video.at[:early, pl.ds((1 - lower) * half, half)], rest_front),
        (video.at[early:, pl.ds((1 - lower) * half, half)], rest_late),
        (weight, staged.at[0:size]),
        (first_bias, first_line),
        (second_bias, second_line),
    )
    copies = [pltpu.make_async_copy(source, target, sems.at[k]) for k, (source, target) in enumerate(pairs)]
    for copy in copies:
        copy.start()
    for copy in copies[5:]:
        copy.wait()
    width = staged.shape[1]
    first = first_line[...]
    first = jnp.concatenate([first, jnp.zeros((1, width - first.shape[1]), first.dtype)], axis=1)
    rows = thirds(first) + thirds(second_line[...])
    rows.append(jnp.zeros((TAIL - len(rows), width), jnp.bfloat16))
    staged[size:] = jnp.concatenate(rows, axis=0)
    for copy in copies[:5]:
        copy.wait()


def join_kernel(kept, taken, latents, sems):
    lower = lower_half()
    half = kept.shape[1]
    copies = [
        pltpu.make_async_copy(part, latents.at[:, pl.ds(place * half, half)], sems.at[k])
        for k, (part, place) in enumerate(((kept, lower), (taken, 1 - lower)))
    ]
    for copy in copies:
        copy.start()
    for copy in copies:
        copy.wait()


def pack_kernel(own, other, inner, outer, bias_first, bias_second):
    core, lower = lax.axis_index("chan"), lower_half()
    known = border_known()
    taps = 3
    rows = taps + 1
    width = own.shape[1]
    size = own.shape[0] - TAIL
    channels = size // taps**3

    def lines(source):
        last = source[size:].astype(jnp.float32)
        added = [last[3 * k : 3 * k + 1] + last[3 * k + 1 : 3 * k + 2] + last[3 * k + 2 : 3 * k + 3] for k in range(2)]
        return added[0][:, :channels], added[1]

    mine, theirs = lines(own), lines(other)
    low = [jnp.where(core == 0, m, t) for m, t in zip(mine, theirs)]
    high = [jnp.where(core == 0, t, m) for m, t in zip(mine, theirs)]
    once = jnp.concatenate([low[0], high[0]], axis=1)
    bias_first[...] = jnp.concatenate([once, once], axis=1)
    bias_second[...] = jnp.concatenate([low[1], high[1]], axis=1)
    for a in range(taps):
        for e in range(taps):
            full = []
            for b in range(taps):
                at = ((a * taps + b) * taps + e) * channels
                mine, theirs = own[at : at + channels], other[at : at + channels]
                low = jnp.where(core == 0, mine, theirs)
                high = jnp.where(core == 0, theirs, mine)
                full.append(jnp.concatenate([low, high], axis=0).T)
            nothing = jnp.zeros_like(full[0])
            across = slice(e * 2 * width, (e + 1) * 2 * width)
            for i in range(rows):
                pair = [full[i - j] if 0 <= i - j < taps else nothing for j in range(2)]
                pair = jnp.concatenate(pair, axis=1)
                upper = i < rows // 2
                at = lax.rem(i + 2 * lower, rows) + a * rows
                inner[pl.ds(pl.multiple_of(at * width, width), width), across] = pair
                at = lax.rem(i + 2 * (1 - lower), rows) + a * rows
                used = known | (lower == (1 if upper else 0))
                outer[pl.ds(pl.multiple_of(at * width, width), width), across] = jnp.where(
                    used, pair, jnp.zeros_like(pair)
                )


def first_layer(tile, frames, packed, bias):
    taps = 3
    rows = taps + 1
    left = jnp.concatenate(
        [
            jnp.concatenate([tile(f + a, k) for f in frames], axis=0)
            for a in range(taps)
            for k in range(rows)
        ],
        axis=1,
    )
    double = packed.shape[1] // taps
    columns = left.shape[0] // len(frames)
    parts = [
        jnp.dot(left, packed[:, e * double : (e + 1) * double], preferred_element_type=jnp.float32)
        for e in range(taps)
    ]
    return silu(shifted_sum(parts, columns) + bias).astype(jnp.bfloat16)


def second_layer(terms, second):
    left = jnp.concatenate([tile for tile, _, _ in terms], axis=1)
    parts = [
        jnp.dot(
            left,
            jnp.concatenate([second[a, b, e] for _, a, b in terms], axis=0),
            preferred_element_type=jnp.float32,
        )
        for e in range(second.shape[2])
    ]
    return shifted_sum(parts, left.shape[0])


def terms_of(tile, frames, late):
    both = [(tile(n, j), a, 1 - late + j) for n, a in frames for j in range(2)]
    return both, [(tile(n, late), a, 2 * (1 - late)) for n, a in frames]


def put_rows(result, target, start, columns, masks):
    width = target.shape[-1]
    for n in range(result.shape[0] // columns):
        for j in range(2):
            row = result[n * columns : (n + 1) * columns, j * width : (j + 1) * width]
            target[start + n, j] = row if masks is None else jnp.where(masks[j], row, jnp.zeros_like(row))


def border_masks():
    lower, known = lower_half(), border_known()
    return [known | (lower != j) for j in range(2)]


def ahead_kernel(front, late, *refs, border):
    *beside, packed, bias, hidden = refs
    half, columns = front.shape[1:3]

    def frame(parts, f):
        return (parts[0], f) if f < parts[0].shape[0] else frame(parts[1:], f - parts[0].shape[0])

    def tile(f, k):
        part, at = frame((front, late) if k < half else beside, f)
        return part[at, k % half]

    count = hidden.shape[0]
    last = lax.axis_index("slab") == lax.axis_size("slab") - 1

    def fill(frames):
        result = first_layer(tile, range(frames), packed, bias[...])
        put_rows(result, hidden, 0, columns, border_masks() if border else None)

    pl.when(jnp.logical_not(last))(lambda: fill(count))

    @pl.when(last)
    def _():
        fill(count - 1)
        hidden[count - 1] = jnp.zeros(hidden.shape[1:], hidden.dtype)


def behind(own, beside, passed, passed_beside, packed, bias, hidden, start, masks):
    early, half, columns = passed.shape[:3]
    follows = lax.axis_index("slab") > 0

    def tile(f, k):
        if f >= early:
            return own[f - early, k] if k < half else beside[f - early, k - half]
        row = passed[f, k] if k < half else passed_beside[f, k - half]
        return jnp.where(follows, row, jnp.zeros_like(row))

    put_rows(first_layer(tile, range(early), packed, bias[...]), hidden, start, columns, masks)


def inner_kernel(own, rest, passed, passed_other, packed, bias, ahead, second, partial, hidden):
    behind(own, rest, passed, passed_other, packed, bias, hidden, 0, None)
    hidden[passed.shape[0]] = ahead[0]

    def store(t, row, value):
        partial[t, row] = value

    add_layers(hidden, lower_half(), second, store)


def add_layers(hidden, late, second, store):
    tile = lambda n, j: hidden[n, j]
    for t, frames in enumerate(([(0, 2)], [(0, 0), (1, 1), (2, 2)])):
        for row, terms in zip((1 - late, late), terms_of(tile, frames, late)):
            store(t, row, second_layer(terms, second))


def finish(value, bias, row, kept, given):
    core = lax.axis_index("chan")
    total = silu(value + bias[...]).astype(jnp.bfloat16)
    portion = kept.shape[-1]
    low, high = total[:, :portion], total[:, portion:]
    kept[row] = jnp.where(core == 0, low, high)
    given[row] = jnp.where(core == 0, high, low)


def outer_kernel(
    own, beyond, passed, passed_beyond, packed, bias, ahead, second, bias_second, partial, kept, given, left, hidden
):
    behind(own, beyond, passed, passed_beyond, packed, bias, hidden, 0, border_masks())
    hidden[passed.shape[0]] = ahead[0]

    def store(t, row, value):
        if t == 0:
            left[row] = partial[t, row] + value
        else:
            finish(partial[t, row] + value, bias_second, row, kept, given)

    add_layers(hidden, 1 - lower_half(), second, store)


def last_kernel(
    handed_inner, handed_outer, second, bias_second, left, kept_second, given_second, kept, given
):
    lower = lower_half()
    follows = lax.axis_index("slab") > 0
    frames = [(0, 0), (1, 1)]
    kept[1] = kept_second[...]
    given[1] = given_second[...]

    @pl.when(follows)
    def _():
        inner_both, inner_one = terms_of(lambda n, j: handed_inner[n, j], frames, lower)
        outer_both, outer_one = terms_of(lambda n, j: handed_outer[n, j], frames, 1 - lower)
        for row, terms in ((1 - lower, inner_both + outer_one), (lower, outer_both + inner_one)):
            finish(left[row] + second_layer(terms, second), bias_second, row, kept.at[0], given.at[0])

    @pl.when(jnp.logical_not(follows))
    def _():
        for row in range(left.shape[0]):
            finish(left[row], bias_second, row, kept.at[0], given.at[0])


def cycle(value, axis):
    count = lax.axis_size(axis)
    return lax.ppermute(value, axis, [(i, (i + 1) % count) for i in range(count)])


def across_border(value):
    clips, tiles = lax.axis_size("clip"), lax.axis_size("tile")
    at = lambda c, t, k: (c * tiles + t) * 2 + k
    pairs = []
    for clip in range(clips):
        for tile in range(tiles - 1):
            core = (tile + 1) % 2
            pairs.append((at(clip, tile, core), at(clip, tile + 1, core)))
            pairs.append((at(clip, tile + 1, core), at(clip, tile, core)))
        if clips > 1:
            for tile, core in ((0, 0), (tiles - 1, tiles % 2)):
                pairs.append((at(clip, tile, core), at((clip + 1) % clips, tile, core)))
    return lax.ppermute(value, ("clip", "tile", "chan"), pairs)


def shards(video, first_weight, first_bias, second_weight, second_bias):
    frames, rows, columns, width = video.shape
    half = rows // 2
    taps = first_weight.shape[0]
    assert half == taps - 1 and frames == 2 * (taps - 1) and lax.axis_size("chan") == 2
    bf16 = jnp.bfloat16
    shape = jax.ShapeDtypeStruct
    small = pl.CostEstimate(flops=1000, bytes_accessed=1000, transcendentals=0)

    def call(kernel, outs, ins, scratch, *operands, out_specs=None, limit=LIMIT):
        return pl.pallas_call(
            kernel,
            out_shape=outs,
            in_specs=ins,
            out_specs=[VMEM] * len(outs) if out_specs is None else out_specs,
            scratch_shapes=scratch,
            compiler_params=pltpu.CompilerParams(vmem_limit_bytes=limit),
            cost_estimate=small,
        )(*operands)

    early = frames // 2
    short = shape((early, half, columns, width), bf16)
    turned = jnp.swapaxes(first_weight, 3, 4).reshape(-1, width)
    far = lambda value: pltpu.with_memory_space_constraint(value, pltpu.HBM)
    front, late, rest_front, rest_late, staged = call(
        stage_kernel,
        [
            pltpu.VMEM(short.shape, bf16),
            pltpu.VMEM(short.shape, bf16),
            pltpu.VMEM(short.shape, bf16),
            pltpu.VMEM(short.shape, bf16),
            pltpu.VMEM((turned.shape[0] + TAIL, width), bf16),
        ],
        [HBM] * 4,
        [
            pltpu.VMEM((1, first_bias.shape[0]), jnp.float32),
            pltpu.VMEM((1, second_bias.shape[0]), jnp.float32),
            pltpu.SemaphoreType.DMA((7,)),
        ],
        far(video), far(turned), far(first_bias.reshape(1, -1)), far(second_bias.reshape(1, -1)),
    )
    beyond_front, beyond_late = across_border(front), across_border(late)
    passed = cycle(late, "slab")
    passed_other = cycle(rest_late, "slab")
    staged_other = cycle(staged, "chan")
    matrix = shape((taps * (taps + 1) * width, taps * 2 * width), bf16)
    channels = second_weight.shape[4]
    packed, packed_outer, bias_first, bias_last = call(
        pack_kernel,
        [matrix, matrix, shape((1, 2 * width), jnp.float32), shape((1, channels), jnp.float32)],
        [VMEM] * 2,
        [],
        staged, staged_other,
    )
    (ahead_inner,) = call(
        functools.partial(ahead_kernel, border=False), [short], [VMEM] * 6, [], front, late, rest_front, rest_late,
        packed, bias_first
    )
    handed_inner = cycle(ahead_inner, "slab")
    passed, _ = lax.optimization_barrier((passed, ahead_inner))
    passed_beyond = across_border(passed)
    (ahead_outer,) = call(
        functools.partial(ahead_kernel, border=True),
        [short],
        [VMEM] * 6,
        [],
        front, late, beyond_front, beyond_late, packed_outer, bias_first,
    )
    handed_outer = cycle(ahead_outer, "slab")
    (partial,) = call(
        inner_kernel,
        [shape((early, half, columns, channels), jnp.float32)],
        [VMEM] * 8,
        [pltpu.VMEM((early + 1, half, columns, width), bf16)],
        front, rest_front, passed, passed_other, packed, bias_first, ahead_inner, second_weight,
    )
    part = shape((half, columns, second_bias.shape[0]), bf16)
    handed_inner, partial = lax.optimization_barrier((handed_inner, partial))
    kept_second, given_second, left = call(
        outer_kernel,
        [part, part, shape((half, columns, channels), jnp.float32)],
        [VMEM] * 10,
        [pltpu.VMEM((early + 1, half, columns, width), bf16)],
        front, beyond_front, passed, passed_beyond, packed_outer, bias_first, ahead_outer, second_weight, bias_last, partial,
    )
    whole = shape((early,) + part.shape, bf16)
    kept, given = call(
        last_kernel,
        [whole, whole],
        [VMEM] * 7,
        [],
        handed_inner, handed_outer, second_weight, bias_last, left, kept_second, given_second,
    )
    (latents,) = call(
        join_kernel,
        [shape((early, rows, columns, second_bias.shape[0]), bf16)],
        [VMEM] * 2,
        [pltpu.SemaphoreType.DMA((2,))],
        kept, cycle(given, "chan"),
        out_specs=[ANY],
    )
    return latents


def solution(mesh):
    placed = (
        P(("clip", "slab"), "tile", None, None),
        P(None, None, None, None, "chan"),
        P("chan"),
        P(),
        P("chan"),
    )
    return jax.shard_map(
        shards,
        mesh=mesh,
        in_specs=placed,
        out_specs=P(("clip", "slab"), "tile", None, "chan"),
        check_vma=False,
    )
```

```python
import functools

import jax
import jax.numpy as jnp
from jax import lax
from jax.experimental import pallas as pl
from jax.experimental.pallas import tpu as pltpu
from jax.sharding import PartitionSpec as P

VMEM = pl.BlockSpec(memory_space=pltpu.VMEM)
ANY = pl.BlockSpec(memory_space=pl.ANY)
HBM = pl.BlockSpec(memory_space=pltpu.HBM)
LIMIT = 20 * 1024 * 1024
TAIL = 16
SPARE = 16


def silu(value):
    half = 0.5 * value
    return half + half * jnp.tanh(half)


def shifted_sum(part, columns):
    def cells(value):
        size, width = value.shape
        value = value.reshape(size // columns, columns, width)
        return value, lax.broadcasted_iota(jnp.int32, (1, columns, width), 1)

    before, cell = cells(part(0))
    total = jnp.where(cell == 0, 0.0, pltpu.roll(before, 1, 1))
    after, cell = cells(part(2))
    total = total + jnp.where(cell == columns - 1, 0.0, pltpu.roll(after, columns - 1, 1))
    here = part(1)
    return here + total.reshape(here.shape)


def lower_half():
    return lax.rem(lax.axis_index("chan") + lax.axis_index("tile"), 2)


def border_known():
    lower, tile = lower_half(), lax.axis_index("tile")
    last = lax.axis_size("tile") - 1
    return jnp.logical_not(jnp.logical_or((lower == 0) & (tile == 0), (lower == 1) & (tile == last)))


def thirds(value):
    high = value.astype(jnp.bfloat16)
    left = value - high.astype(jnp.float32)
    middle = left.astype(jnp.bfloat16)
    return [high, middle, (left - middle.astype(jnp.float32)).astype(jnp.bfloat16)]


def stage_kernel(video, weight, first_bias, second_bias, front, late, rest_front, rest_late, staged, first_line, second_line, sems):
    lower = lower_half()
    early, half = front.shape[:2]
    size = weight.shape[0]
    pairs = (
        (first_bias, first_line),
        (second_bias, second_line),
        (weight, staged.at[0:size]),
        (video.at[early:, pl.ds(lower * half, half)], late),
        (video.at[:early, pl.ds(lower * half, half)], front),
        (video.at[early:, pl.ds((1 - lower) * half, half)], rest_late),
        (video.at[:early, pl.ds((1 - lower) * half, half)], rest_front),
    )
    copies = [pltpu.make_async_copy(source, target, sems.at[k]) for k, (source, target) in enumerate(pairs)]
    for copy in copies:
        copy.start()
    for copy in copies[:2]:
        copy.wait()
    width = staged.shape[1]
    first = first_line[...]
    first = jnp.concatenate([first, jnp.zeros((1, width - first.shape[1]), first.dtype)], axis=1)
    rows = thirds(first) + thirds(second_line[...])
    rows.append(jnp.zeros((TAIL - len(rows), width), jnp.bfloat16))
    staged[size:] = jnp.concatenate(rows, axis=0)
    for copy in copies[2:]:
        copy.wait()


def join_kernel(kept, taken, latents, sems):
    lower = lower_half()
    half = kept.shape[1]
    copies = [
        pltpu.make_async_copy(part, latents.at[:, pl.ds(place * half, half)], sems.at[k])
        for k, (part, place) in enumerate(((kept, lower), (taken, 1 - lower)))
    ]
    for copy in copies:
        copy.start()
    for copy in copies:
        copy.wait()


def pack_kernel(own, other, packed, bias_first, bias_second):
    core, lower = lax.axis_index("chan"), lower_half()
    taps = 3
    rows = taps + 1
    width = own.shape[1]
    size = own.shape[0] - TAIL
    channels = size // taps**3

    def lines(source):
        last = source[size:].astype(jnp.float32)
        added = [last[3 * k : 3 * k + 1] + last[3 * k + 1 : 3 * k + 2] + last[3 * k + 2 : 3 * k + 3] for k in range(2)]
        return added[0][:, :channels], added[1]

    mine, theirs = lines(own), lines(other)
    low = [jnp.where(core == 0, m, t) for m, t in zip(mine, theirs)]
    high = [jnp.where(core == 0, t, m) for m, t in zip(mine, theirs)]
    once = jnp.concatenate([low[0], high[0]], axis=1)
    bias_first[...] = jnp.concatenate([once, once], axis=1)
    bias_second[...] = jnp.concatenate([low[1], high[1]], axis=1)
    for a in range(taps):
        for e in range(taps):
            full = []
            for b in range(taps):
                at = ((a * taps + b) * taps + e) * channels
                mine, theirs = own[at : at + channels], other[at : at + channels]
                low = jnp.where(core == 0, mine, theirs)
                high = jnp.where(core == 0, theirs, mine)
                full.append(jnp.concatenate([low, high], axis=0).T)
            nothing = jnp.zeros_like(full[0])
            across = slice(e * 2 * width, (e + 1) * 2 * width)
            for i in range(rows):
                pair = [full[i - j] if 0 <= i - j < taps else nothing for j in range(2)]
                pair = jnp.concatenate(pair, axis=1)
                at = lax.rem(i + 2 * lower, rows) + a * rows
                packed[pl.ds(pl.multiple_of(at * width, width), width), across] = pair


def first_layer(tile, frames, packed, bias):
    taps = 3
    rows = taps + 1
    left = jnp.concatenate(
        [
            jnp.concatenate([tile(f + a, k) for f in frames], axis=0)
            for a in range(taps)
            for k in range(rows)
        ],
        axis=1,
    )
    double = packed.shape[1] // taps
    columns = left.shape[0] // len(frames)
    part = lambda e: jnp.dot(left, packed[:, e * double : (e + 1) * double], preferred_element_type=jnp.float32)
    return silu(shifted_sum(part, columns) + bias).astype(jnp.bfloat16)


def second_layer(terms, second):
    left = jnp.concatenate([tile for tile, _, _ in terms], axis=1)

    def part(e):
        right = jnp.concatenate([second[a, b, e] for _, a, b in terms], axis=0)
        return jnp.dot(left, right, preferred_element_type=jnp.float32)

    return shifted_sum(part, left.shape[0])


def terms_of(tile, frames, late):
    both = [(tile(n, j), a, 1 - late + j) for n, a in frames for j in range(2)]
    return both, [(tile(n, late), a, 2 * (1 - late)) for n, a in frames]


def put_rows(result, target, start, columns, masks):
    width = target.shape[-1]
    for n in range(result.shape[0] // columns):
        for j in range(2):
            row = result[n * columns : (n + 1) * columns, j * width : (j + 1) * width]
            target[start + n, j] = row if masks is None else jnp.where(masks[j], row, jnp.zeros_like(row))


def border_masks():
    lower, known = lower_half(), border_known()
    return [known | (lower != j) for j in range(2)]


def last_slab():
    return lax.axis_index("slab") == lax.axis_size("slab") - 1


def masked(row, *conditions):
    for condition in conditions:
        row = jnp.where(condition, row, jnp.zeros_like(row))
    return row


def ahead_kernel(*refs, border):
    early_first, late_first, early_second, late_second, packed, bias, hidden, *sent = refs
    early, half, columns = early_first.shape[:3]
    unknown = [border_known()] if border else []

    def tile(f, k):
        first, second = (early_first, early_second) if f < early else (late_first, late_second)
        return masked(first[f % early, k], *unknown) if k < half else second[f % early, k - half]

    @pl.when(jnp.logical_not(last_slab()))
    def _():
        result = first_layer(tile, range(hidden.shape[0]), packed, bias[...])
        put_rows(result, hidden, 0, columns, border_masks() if border else None)
        for target in sent:
            size = target.shape[0] - SPARE
            target[:size] = hidden[...].reshape(size, target.shape[1])
            target[size:] = jnp.zeros((SPARE, target.shape[1]), target.dtype)

    @pl.when(last_slab())
    def _():
        for target in (hidden, *sent):
            target[...] = jnp.zeros(target.shape, target.dtype)


def behind(first, second, passed_first, passed_second, packed, bias, ahead, hidden, border):
    early, half, columns = passed_first.shape[:3]
    follows = lax.axis_index("slab") > 0
    unknown = [border_known()] if border else []

    def tile(f, k):
        if f >= early:
            part = (first if k < half else second)[f // early - 1]
            return masked(part[f % early, k % half], *(unknown if k < half else []))
        if k < half:
            return masked(passed_first[f, k], follows, *unknown)
        return masked(passed_second[f, k - half], follows)

    def fill(frames):
        result = first_layer(tile, range(frames), packed, bias[...])
        put_rows(result, hidden, 0, columns, border_masks() if border else None)

    @pl.when(jnp.logical_not(last_slab()))
    def _():
        fill(early)
        hidden[early] = ahead[0]

    pl.when(last_slab())(lambda: fill(early + 1))


def inner_kernel(
    front, late, rest_front, rest_late, passed, passed_other, packed, bias, ahead, second, partial, hidden
):
    halves = (front, late), (rest_front, rest_late)
    behind(*halves, passed, passed_other, packed, bias, ahead, hidden, False)

    def store(t, row, value):
        partial[t, row] = value

    add_layers(hidden, lower_half(), second, store)


def add_layers(hidden, late, second, store):
    tile = lambda n, j: hidden[n, j]
    for t, frames in enumerate(([(0, 2)], [(0, 0), (1, 1), (2, 2)])):
        for row, terms in zip((1 - late, late), terms_of(tile, frames, late)):
            store(t, row, second_layer(terms, second))


def finish(value, bias, row, kept, given):
    core = lax.axis_index("chan")
    total = silu(value + bias[...]).astype(jnp.bfloat16)
    portion = kept.shape[-1]
    low, high = total[:, :portion], total[:, portion:]
    kept[row] = jnp.where(core == 0, low, high)
    given[row] = jnp.where(core == 0, high, low)


def outer_kernel(
    front, late, beyond_front, beyond_late, passed, passed_beyond, packed, bias, ahead, second, bias_second, partial,
    kept, given, left, hidden,
):
    halves = (beyond_front, beyond_late), (front, late)
    behind(*halves, passed_beyond, passed, packed, bias, ahead, hidden, True)

    def store(t, row, value):
        if t == 0:
            left[row] = partial[t, row] + value
        else:
            finish(partial[t, row] + value, bias_second, row, kept, given)

    add_layers(hidden, 1 - lower_half(), second, store)


def last_kernel(
    handed_inner, handed_outer, second, bias_second, left, kept_second, given_second, kept, given
):
    lower = lower_half()
    follows = lax.axis_index("slab") > 0
    frames = [(0, 0), (1, 1)]
    kept[1] = kept_second[...]
    given[1] = given_second[...]

    @pl.when(follows)
    def _():
        half, columns = handed_outer.shape[1:3]

        def inner(n, j):
            return handed_inner[pl.ds(pl.multiple_of((n * half + j) * columns, columns), columns)]

        inner_both, inner_one = terms_of(inner, frames, lower)
        outer_both, outer_one = terms_of(lambda n, j: handed_outer[n, j], frames, 1 - lower)
        for row, terms in ((1 - lower, inner_both + outer_one), (lower, outer_both + inner_one)):
            finish(left[row] + second_layer(terms, second), bias_second, row, kept.at[0], given.at[0])

    @pl.when(jnp.logical_not(follows))
    def _():
        for row in range(left.shape[0]):
            finish(left[row], bias_second, row, kept.at[0], given.at[0])


def cycle(value, axis):
    count = lax.axis_size(axis)
    return lax.ppermute(value, axis, [(i, (i + 1) % count) for i in range(count)])


def across_border(value):
    clips, tiles = lax.axis_size("clip"), lax.axis_size("tile")
    at = lambda c, t, k: (c * tiles + t) * 2 + k
    pairs = []
    for clip in range(clips):
        for tile in range(tiles - 1):
            core = (tile + 1) % 2
            pairs.append((at(clip, tile, core), at(clip, tile + 1, core)))
            pairs.append((at(clip, tile + 1, core), at(clip, tile, core)))
        if clips > 1:
            for tile, core in ((0, 0), (tiles - 1, tiles % 2)):
                pairs.append((at(clip, tile, core), at((clip + 1) % clips, tile, core)))
    return lax.ppermute(value, ("clip", "tile", "chan"), pairs)


def shards(video, first_weight, first_bias, second_weight, second_bias):
    frames, rows, columns, width = video.shape
    half = rows // 2
    taps = first_weight.shape[0]
    assert half == taps - 1 and frames == 2 * (taps - 1) and lax.axis_size("chan") == 2
    bf16 = jnp.bfloat16
    shape = jax.ShapeDtypeStruct
    small = pl.CostEstimate(flops=1000, bytes_accessed=1000, transcendentals=0)

    def call(kernel, outs, ins, scratch, *operands, out_specs=None, limit=LIMIT):
        return pl.pallas_call(
            kernel,
            out_shape=outs,
            in_specs=ins,
            out_specs=[VMEM] * len(outs) if out_specs is None else out_specs,
            scratch_shapes=scratch,
            compiler_params=pltpu.CompilerParams(vmem_limit_bytes=limit),
            cost_estimate=small,
        )(*operands)

    early = frames // 2
    short = shape((early, half, columns, width), bf16)
    turned = jnp.swapaxes(first_weight, 3, 4).reshape(-1, width)
    far = lambda value: pltpu.with_memory_space_constraint(value, pltpu.HBM)
    front, late, rest_front, rest_late, staged = call(
        stage_kernel,
        [
            pltpu.VMEM(short.shape, bf16),
            pltpu.VMEM(short.shape, bf16),
            pltpu.VMEM(short.shape, bf16),
            pltpu.VMEM(short.shape, bf16),
            pltpu.VMEM((turned.shape[0] + TAIL, width), bf16),
        ],
        [HBM] * 4,
        [
            pltpu.VMEM((1, first_bias.shape[0]), jnp.float32),
            pltpu.VMEM((1, second_bias.shape[0]), jnp.float32),
            pltpu.SemaphoreType.DMA((7,)),
        ],
        far(video), far(turned), far(first_bias.reshape(1, -1)), far(second_bias.reshape(1, -1)),
    )
    beyond_front, beyond_late = across_border(front), across_border(late)
    passed = cycle(late, "slab")
    staged_other = cycle(staged, "chan")
    matrix = shape((taps * (taps + 1) * width, taps * 2 * width), bf16)
    channels = second_weight.shape[4]
    packed, bias_first, bias_last = call(
        pack_kernel,
        [matrix, shape((1, 2 * width), jnp.float32), shape((1, channels), jnp.float32)],
        [VMEM] * 2,
        [],
        staged, staged_other,
    )
    ahead_inner, sent = call(
        functools.partial(ahead_kernel, border=False),
        [short, shape((early * half * columns + SPARE, width), bf16)],
        [VMEM] * 6, [], front, late, rest_front, rest_late,
        packed, bias_first
    )
    handed_inner = cycle(sent, "slab")
    passed, _ = lax.optimization_barrier((passed, ahead_inner))
    passed_other = cycle(passed, "chan")
    passed_beyond = across_border(passed)
    (ahead_outer,) = call(
        functools.partial(ahead_kernel, border=True),
        [short],
        [VMEM] * 6,
        [],
        beyond_front, beyond_late, front, late, packed, bias_first,
    )
    handed_outer = cycle(ahead_outer, "slab")
    (partial,) = call(
        inner_kernel,
        [shape((early, half, columns, channels), jnp.float32)],
        [VMEM] * 10,
        [pltpu.VMEM((early + 1, half, columns, width), bf16)],
        front, late, rest_front, rest_late, passed, passed_other, packed, bias_first, ahead_inner, second_weight,
    )
    part = shape((half, columns, second_bias.shape[0]), bf16)
    handed_inner, partial = lax.optimization_barrier((handed_inner, partial))
    kept_second, given_second, left = call(
        outer_kernel,
        [part, part, shape((half, columns, channels), jnp.float32)],
        [VMEM] * 12,
        [pltpu.VMEM((early + 1, half, columns, width), bf16)],
        front, late, beyond_front, beyond_late, passed, passed_beyond, packed, bias_first, ahead_outer, second_weight, bias_last, partial,
    )
    whole = shape((early,) + part.shape, bf16)
    kept, given = call(
        last_kernel,
        [whole, whole],
        [VMEM] * 7,
        [],
        handed_inner, handed_outer, second_weight, bias_last, left, kept_second, given_second,
    )
    (latents,) = call(
        join_kernel,
        [shape((early, rows, columns, second_bias.shape[0]), bf16)],
        [VMEM] * 2,
        [pltpu.SemaphoreType.DMA((2,))],
        kept, cycle(given, "chan"),
        out_specs=[ANY],
    )
    return latents


def solution(mesh):
    placed = (
        P(("clip", "slab"), "tile", None, None),
        P(None, None, None, None, "chan"),
        P("chan"),
        P(),
        P("chan"),
    )
    return jax.shard_map(
        shards,
        mesh=mesh,
        in_specs=placed,
        out_specs=P(("clip", "slab"), "tile", None, "chan"),
        check_vma=False,
    )
```

```python
import functools

import jax
import jax.numpy as jnp
from jax import lax
from jax.experimental import pallas as pl
from jax.experimental.pallas import tpu as pltpu
from jax.sharding import PartitionSpec as P

VMEM = pl.BlockSpec(memory_space=pltpu.VMEM)
ANY = pl.BlockSpec(memory_space=pl.ANY)
HBM = pl.BlockSpec(memory_space=pltpu.HBM)
LIMIT = 20 * 1024 * 1024
TAIL = 16
SPARE = 16


def silu(value):
    half = 0.5 * value
    return half + half * jnp.tanh(half)


def shifted_sum(part, columns):
    def cells(value):
        size, width = value.shape
        value = value.reshape(size // columns, columns, width)
        return value, lax.broadcasted_iota(jnp.int32, (1, columns, width), 1)

    before, cell = cells(part(0))
    total = jnp.where(cell == 0, 0.0, pltpu.roll(before, 1, 1))
    after, cell = cells(part(2))
    total = total + jnp.where(cell == columns - 1, 0.0, pltpu.roll(after, columns - 1, 1))
    here = part(1)
    return here + total.reshape(here.shape)


def lower_half():
    return lax.rem(lax.axis_index("chan") + lax.axis_index("tile"), 2)


def border_known():
    lower, tile = lower_half(), lax.axis_index("tile")
    last = lax.axis_size("tile") - 1
    return jnp.logical_not(jnp.logical_or((lower == 0) & (tile == 0), (lower == 1) & (tile == last)))


def thirds(value):
    high = value.astype(jnp.bfloat16)
    left = value - high.astype(jnp.float32)
    middle = left.astype(jnp.bfloat16)
    return [high, middle, (left - middle.astype(jnp.float32)).astype(jnp.bfloat16)]


def stage_kernel(video, weight, first_bias, second_bias, front, late, rest_front, rest_late, staged, first_line, second_line, sems):
    lower = lower_half()
    early, half = front.shape[:2]
    size = weight.shape[0]
    pairs = (
        (first_bias, first_line),
        (second_bias, second_line),
        (weight, staged.at[0:size]),
        (video.at[early:, pl.ds(lower * half, half)], late),
        (video.at[:early, pl.ds(lower * half, half)], front),
        (video.at[early:, pl.ds((1 - lower) * half, half)], rest_late),
        (video.at[:early, pl.ds((1 - lower) * half, half)], rest_front),
    )
    copies = [pltpu.make_async_copy(source, target, sems.at[k]) for k, (source, target) in enumerate(pairs)]
    for copy in copies:
        copy.start()
    for copy in copies[:2]:
        copy.wait()
    width = staged.shape[1]
    first = first_line[...]
    first = jnp.concatenate([first, jnp.zeros((1, width - first.shape[1]), first.dtype)], axis=1)
    rows = thirds(first) + thirds(second_line[...])
    rows.append(jnp.zeros((TAIL - len(rows), width), jnp.bfloat16))
    staged[size:] = jnp.concatenate(rows, axis=0)
    for copy in copies[2:]:
        copy.wait()


def join_kernel(*refs):
    *parts, latents, sems = refs
    lower = lower_half()
    half = parts[0].shape[0]
    copies = []
    for k, part in enumerate(parts):
        place = lower if k % 2 == 0 else 1 - lower
        copies.append(pltpu.make_async_copy(part, latents.at[k // 2, pl.ds(place * half, half)], sems.at[k]))
    for copy in copies:
        copy.start()
    for copy in copies:
        copy.wait()


def pack_kernel(own, other, packed, bias_first, bias_second):
    core, lower = lax.axis_index("chan"), lower_half()
    taps = 3
    rows = taps + 1
    width = own.shape[1]
    size = own.shape[0] - TAIL
    channels = size // taps**3

    def lines(source):
        last = source[size:].astype(jnp.float32)
        added = [last[3 * k : 3 * k + 1] + last[3 * k + 1 : 3 * k + 2] + last[3 * k + 2 : 3 * k + 3] for k in range(2)]
        return added[0][:, :channels], added[1]

    mine, theirs = lines(own), lines(other)
    low = [jnp.where(core == 0, m, t) for m, t in zip(mine, theirs)]
    high = [jnp.where(core == 0, t, m) for m, t in zip(mine, theirs)]
    once = jnp.concatenate([low[0], high[0]], axis=1)
    bias_first[...] = jnp.concatenate([once, once], axis=1)
    bias_second[...] = jnp.concatenate([low[1], high[1]], axis=1)
    for a in range(taps):
        for e in range(taps):
            full = []
            for b in range(taps):
                at = ((a * taps + b) * taps + e) * channels
                mine, theirs = own[at : at + channels], other[at : at + channels]
                low = jnp.where(core == 0, mine, theirs)
                high = jnp.where(core == 0, theirs, mine)
                full.append(jnp.concatenate([low, high], axis=0).T)
            nothing = jnp.zeros_like(full[0])
            across = slice(e * 2 * width, (e + 1) * 2 * width)
            for i in range(rows):
                pair = [full[i - j] if 0 <= i - j < taps else nothing for j in range(2)]
                pair = jnp.concatenate(pair, axis=1)
                at = lax.rem(i + 2 * lower, rows) + a * rows
                packed[pl.ds(pl.multiple_of(at * width, width), width), across] = pair


def first_layer(tile, frames, packed, bias):
    taps = 3
    rows = taps + 1
    left = jnp.concatenate(
        [
            jnp.concatenate([tile(f + a, k) for f in frames], axis=0)
            for a in range(taps)
            for k in range(rows)
        ],
        axis=1,
    )
    double = packed.shape[1] // taps
    columns = left.shape[0] // len(frames)
    part = lambda e: jnp.dot(left, packed[:, e * double : (e + 1) * double], preferred_element_type=jnp.float32)
    return silu(shifted_sum(part, columns) + bias).astype(jnp.bfloat16)


def second_layer(terms, second):
    left = jnp.concatenate([tile for tile, _, _ in terms], axis=1)

    def part(e):
        right = jnp.concatenate([second[a, b, e] for _, a, b in terms], axis=0)
        return jnp.dot(left, right, preferred_element_type=jnp.float32)

    return shifted_sum(part, left.shape[0])


def terms_of(tile, frames, late):
    both = [(tile(n, j), a, 1 - late + j) for n, a in frames for j in range(2)]
    return both, [(tile(n, late), a, 2 * (1 - late)) for n, a in frames]


def put_rows(result, target, start, columns, masks):
    width = target.shape[-1]
    for n in range(result.shape[0] // columns):
        for j in range(2):
            row = result[n * columns : (n + 1) * columns, j * width : (j + 1) * width]
            target[start + n, j] = row if masks is None else jnp.where(masks[j], row, jnp.zeros_like(row))


def border_masks():
    lower, known = lower_half(), border_known()
    return [known | (lower != j) for j in range(2)]


def last_slab():
    return lax.axis_index("slab") == lax.axis_size("slab") - 1


def masked(row, *conditions):
    for condition in conditions:
        row = jnp.where(condition, row, jnp.zeros_like(row))
    return row


def ahead_kernel(*refs, border):
    early_first, late_first, early_second, late_second, packed, bias, hidden, *sent = refs
    early, half, columns = early_first.shape[:3]
    unknown = [border_known()] if border else []

    def tile(f, k):
        first, second = (early_first, early_second) if f < early else (late_first, late_second)
        return masked(first[f % early, k], *unknown) if k < half else second[f % early, k - half]

    @pl.when(jnp.logical_not(last_slab()))
    def _():
        result = first_layer(tile, range(hidden.shape[0]), packed, bias[...])
        put_rows(result, hidden, 0, columns, border_masks() if border else None)
        for target in sent:
            size = target.shape[0] - SPARE
            target[:size] = hidden[...].reshape(size, target.shape[1])
            target[size:] = jnp.zeros((SPARE, target.shape[1]), target.dtype)

    @pl.when(last_slab())
    def _():
        for target in (hidden, *sent):
            target[...] = jnp.zeros(target.shape, target.dtype)


def behind(first, second, passed_first, passed_second, packed, bias, ahead, hidden, border):
    early, half, columns = passed_first.shape[:3]
    follows = lax.axis_index("slab") > 0
    unknown = [border_known()] if border else []

    def tile(f, k):
        if f >= early:
            part = (first if k < half else second)[f // early - 1]
            return masked(part[f % early, k % half], *(unknown if k < half else []))
        if k < half:
            return masked(passed_first[f, k], follows, *unknown)
        return masked(passed_second[f, k - half], follows)

    def fill(frames):
        result = first_layer(tile, range(frames), packed, bias[...])
        put_rows(result, hidden, 0, columns, border_masks() if border else None)

    @pl.when(jnp.logical_not(last_slab()))
    def _():
        fill(early)
        hidden[early] = ahead[0]

    pl.when(last_slab())(lambda: fill(early + 1))


def inner_kernel(
    front, late, rest_front, rest_late, passed, passed_other, packed, bias, ahead, second, partial, hidden
):
    halves = (front, late), (rest_front, rest_late)
    behind(*halves, passed, passed_other, packed, bias, ahead, hidden, False)

    def store(t, row, value):
        partial[t, row] = value

    add_layers(hidden, lower_half(), second, store)


def add_layers(hidden, late, second, store):
    tile = lambda n, j: hidden[n, j]
    for t, frames in enumerate(([(0, 2)], [(0, 0), (1, 1), (2, 2)])):
        for row, terms in zip((1 - late, late), terms_of(tile, frames, late)):
            store(t, row, second_layer(terms, second))


def finish(value, bias, row, kept, given):
    core = lax.axis_index("chan")
    total = silu(value + bias[...]).astype(jnp.bfloat16)
    portion = kept.shape[-1]
    low, high = total[:, :portion], total[:, portion:]
    kept[row] = jnp.where(core == 0, low, high)
    given[row] = jnp.where(core == 0, high, low)


def outer_kernel(
    front, late, beyond_front, beyond_late, passed, passed_beyond, packed, bias, ahead, second, bias_second, partial,
    kept, given, left, hidden,
):
    halves = (beyond_front, beyond_late), (front, late)
    behind(*halves, passed_beyond, passed, packed, bias, ahead, hidden, True)

    def store(t, row, value):
        if t == 0:
            left[row] = partial[t, row] + value
        else:
            finish(partial[t, row] + value, bias_second, row, kept, given)

    add_layers(hidden, 1 - lower_half(), second, store)


def last_kernel(
    handed_inner, handed_outer, second, bias_second, left, kept, given
):
    lower = lower_half()
    follows = lax.axis_index("slab") > 0
    frames = [(0, 0), (1, 1)]

    @pl.when(follows)
    def _():
        half, columns = handed_outer.shape[1:3]

        def inner(n, j):
            return handed_inner[pl.ds(pl.multiple_of((n * half + j) * columns, columns), columns)]

        inner_both, inner_one = terms_of(inner, frames, lower)
        outer_both, outer_one = terms_of(lambda n, j: handed_outer[n, j], frames, 1 - lower)
        for row, terms in ((1 - lower, inner_both + outer_one), (lower, outer_both + inner_one)):
            finish(left[row] + second_layer(terms, second), bias_second, row, kept, given)

    @pl.when(jnp.logical_not(follows))
    def _():
        for row in range(left.shape[0]):
            finish(left[row], bias_second, row, kept, given)


def cycle(value, axis):
    count = lax.axis_size(axis)
    return lax.ppermute(value, axis, [(i, (i + 1) % count) for i in range(count)])


def across_border(value):
    clips, tiles = lax.axis_size("clip"), lax.axis_size("tile")
    at = lambda c, t, k: (c * tiles + t) * 2 + k
    pairs = []
    for clip in range(clips):
        for tile in range(tiles - 1):
            core = (tile + 1) % 2
            pairs.append((at(clip, tile, core), at(clip, tile + 1, core)))
            pairs.append((at(clip, tile + 1, core), at(clip, tile, core)))
        if clips > 1:
            for tile, core in ((0, 0), (tiles - 1, tiles % 2)):
                pairs.append((at(clip, tile, core), at((clip + 1) % clips, tile, core)))
    return lax.ppermute(value, ("clip", "tile", "chan"), pairs)


def shards(video, first_weight, first_bias, second_weight, second_bias):
    frames, rows, columns, width = video.shape
    half = rows // 2
    taps = first_weight.shape[0]
    assert half == taps - 1 and frames == 2 * (taps - 1) and lax.axis_size("chan") == 2
    bf16 = jnp.bfloat16
    shape = jax.ShapeDtypeStruct
    small = pl.CostEstimate(flops=1000, bytes_accessed=1000, transcendentals=0)

    def call(kernel, outs, ins, scratch, *operands, out_specs=None, limit=LIMIT):
        return pl.pallas_call(
            kernel,
            out_shape=outs,
            in_specs=ins,
            out_specs=[VMEM] * len(outs) if out_specs is None else out_specs,
            scratch_shapes=scratch,
            compiler_params=pltpu.CompilerParams(vmem_limit_bytes=limit),
            cost_estimate=small,
        )(*operands)

    early = frames // 2
    short = shape((early, half, columns, width), bf16)
    turned = jnp.swapaxes(first_weight, 3, 4).reshape(-1, width)
    far = lambda value: pltpu.with_memory_space_constraint(value, pltpu.HBM)
    front, late, rest_front, rest_late, staged = call(
        stage_kernel,
        [
            pltpu.VMEM(short.shape, bf16),
            pltpu.VMEM(short.shape, bf16),
            pltpu.VMEM(short.shape, bf16),
            pltpu.VMEM(short.shape, bf16),
            pltpu.VMEM((turned.shape[0] + TAIL, width), bf16),
        ],
        [HBM] * 4,
        [
            pltpu.VMEM((1, first_bias.shape[0]), jnp.float32),
            pltpu.VMEM((1, second_bias.shape[0]), jnp.float32),
            pltpu.SemaphoreType.DMA((7,)),
        ],
        far(video), far(turned), far(first_bias.reshape(1, -1)), far(second_bias.reshape(1, -1)),
    )
    beyond_front, beyond_late = across_border(front), across_border(late)
    passed = cycle(late, "slab")
    staged_other = cycle(staged, "chan")
    matrix = shape((taps * (taps + 1) * width, taps * 2 * width), bf16)
    channels = second_weight.shape[4]
    packed, bias_first, bias_last = call(
        pack_kernel,
        [matrix, shape((1, 2 * width), jnp.float32), shape((1, channels), jnp.float32)],
        [VMEM] * 2,
        [],
        staged, staged_other,
    )
    ahead_inner, sent = call(
        functools.partial(ahead_kernel, border=False),
        [short, shape((early * half * columns + SPARE, width), bf16)],
        [VMEM] * 6, [], front, late, rest_front, rest_late,
        packed, bias_first
    )
    handed_inner = cycle(sent, "slab")
    passed, _ = lax.optimization_barrier((passed, ahead_inner))
    passed_other = cycle(passed, "chan")
    passed_beyond = across_border(passed)
    (ahead_outer,) = call(
        functools.partial(ahead_kernel, border=True),
        [short],
        [VMEM] * 6,
        [],
        beyond_front, beyond_late, front, late, packed, bias_first,
    )
    handed_outer = cycle(ahead_outer, "slab")
    (partial,) = call(
        inner_kernel,
        [shape((early, half, columns, channels), jnp.float32)],
        [VMEM] * 10,
        [pltpu.VMEM((early + 1, half, columns, width), bf16)],
        front, late, rest_front, rest_late, passed, passed_other, packed, bias_first, ahead_inner, second_weight,
    )
    part = shape((half, columns, second_bias.shape[0]), bf16)
    handed_inner, partial = lax.optimization_barrier((handed_inner, partial))
    kept_second, given_second, left = call(
        outer_kernel,
        [part, part, shape((half, columns, channels), jnp.float32)],
        [VMEM] * 12,
        [pltpu.VMEM((early + 1, half, columns, width), bf16)],
        front, late, beyond_front, beyond_late, passed, passed_beyond, packed, bias_first, ahead_outer, second_weight, bias_last, partial,
    )
    taken_second = cycle(given_second, "chan")
    left, taken_second = lax.optimization_barrier((left, taken_second))
    kept_first, given_first = call(
        last_kernel, [part, part], [VMEM] * 5, [], handed_inner, handed_outer, second_weight, bias_last, left
    )
    (latents,) = call(
        join_kernel,
        [shape((early, rows, columns, second_bias.shape[0]), bf16)],
        [VMEM] * 4,
        [pltpu.SemaphoreType.DMA((4,))],
        kept_first, cycle(given_first, "chan"), kept_second, taken_second,
        out_specs=[ANY],
    )
    return latents


def solution(mesh):
    placed = (
        P(("clip", "slab"), "tile", None, None),
        P(None, None, None, None, "chan"),
        P("chan"),
        P(),
        P("chan"),
    )
    return jax.shard_map(
        shards,
        mesh=mesh,
        in_specs=placed,
        out_specs=P(("clip", "slab"), "tile", None, "chan"),
        check_vma=False,
    )
```

```python
import functools

import jax
import jax.numpy as jnp
from jax import lax
from jax.experimental import pallas as pl
from jax.experimental.pallas import tpu as pltpu
from jax.sharding import PartitionSpec as P

VMEM = pl.BlockSpec(memory_space=pltpu.VMEM)
ANY = pl.BlockSpec(memory_space=pl.ANY)
HBM = pl.BlockSpec(memory_space=pltpu.HBM)
LIMIT = 20 * 1024 * 1024
TAIL = 16
SPARE = 16


def silu(value):
    half = 0.5 * value
    return half + half * jnp.tanh(half)


def shifted_sum(part, columns):
    def cells(value):
        size, width = value.shape
        value = value.reshape(size // columns, columns, width)
        return value, lax.broadcasted_iota(jnp.int32, (1, columns, width), 1)

    before, cell = cells(part(0))
    total = jnp.where(cell == 0, 0.0, pltpu.roll(before, 1, 1))
    after, cell = cells(part(2))
    total = total + jnp.where(cell == columns - 1, 0.0, pltpu.roll(after, columns - 1, 1))
    here = part(1)
    return here + total.reshape(here.shape)


def lower_half():
    return lax.rem(lax.axis_index("chan") + lax.axis_index("tile"), 2)


def border_known():
    lower, tile = lower_half(), lax.axis_index("tile")
    last = lax.axis_size("tile") - 1
    return jnp.logical_not(jnp.logical_or((lower == 0) & (tile == 0), (lower == 1) & (tile == last)))


def thirds(value):
    high = value.astype(jnp.bfloat16)
    left = value - high.astype(jnp.float32)
    middle = left.astype(jnp.bfloat16)
    return [high, middle, (left - middle.astype(jnp.float32)).astype(jnp.bfloat16)]


def stage_kernel(video, weight, first_bias, second_bias, front, late, rest, staged, first_line, second_line, sems):
    lower = lower_half()
    early, half = front.shape[:2]
    size = weight.shape[0]
    pairs = (
        (first_bias, first_line),
        (second_bias, second_line),
        (weight, staged.at[0:size]),
        (video.at[early:, pl.ds(lower * half, half)], late),
        (video.at[:early, pl.ds(lower * half, half)], front),
        (video.at[:, pl.ds((1 - lower) * half, half)], rest),
    )
    copies = [pltpu.make_async_copy(source, target, sems.at[k]) for k, (source, target) in enumerate(pairs)]
    for copy in copies:
        copy.start()
    for copy in copies[:2]:
        copy.wait()
    width = staged.shape[1]
    first = first_line[...]
    first = jnp.concatenate([first, jnp.zeros((1, width - first.shape[1]), first.dtype)], axis=1)
    rows = thirds(first) + thirds(second_line[...])
    rows.append(jnp.zeros((TAIL - len(rows), width), jnp.bfloat16))
    staged[size:] = jnp.concatenate(rows, axis=0)
    for copy in copies[2:]:
        copy.wait()


def join_kernel(*refs):
    *parts, latents, sems = refs
    lower = lower_half()
    half = parts[0].shape[0]
    copies = []
    for k, part in enumerate(parts):
        place = lower if k % 2 == 0 else 1 - lower
        copies.append(pltpu.make_async_copy(part, latents.at[k // 2, pl.ds(place * half, half)], sems.at[k]))
    for copy in copies:
        copy.start()
    for copy in copies:
        copy.wait()


def pack_kernel(own, other, packed, bias_first, bias_second):
    core, lower = lax.axis_index("chan"), lower_half()
    taps = 3
    rows = taps + 1
    width = own.shape[1]
    size = own.shape[0] - TAIL
    channels = size // taps**3

    def lines(source):
        last = source[size:].astype(jnp.float32)
        added = [last[3 * k : 3 * k + 1] + last[3 * k + 1 : 3 * k + 2] + last[3 * k + 2 : 3 * k + 3] for k in range(2)]
        return added[0][:, :channels], added[1]

    mine, theirs = lines(own), lines(other)
    low = [jnp.where(core == 0, m, t) for m, t in zip(mine, theirs)]
    high = [jnp.where(core == 0, t, m) for m, t in zip(mine, theirs)]
    once = jnp.concatenate([low[0], high[0]], axis=1)
    bias_first[...] = jnp.concatenate([once, once], axis=1)
    bias_second[...] = jnp.concatenate([low[1], high[1]], axis=1)
    for a in range(taps):
        for e in range(taps):
            full = []
            for b in range(taps):
                at = ((a * taps + b) * taps + e) * channels
                mine, theirs = own[at : at + channels], other[at : at + channels]
                low = jnp.where(core == 0, mine, theirs)
                high = jnp.where(core == 0, theirs, mine)
                full.append(jnp.concatenate([low, high], axis=0).T)
            nothing = jnp.zeros_like(full[0])
            across = slice(e * 2 * width, (e + 1) * 2 * width)
            for i in range(rows):
                pair = [full[i - j] if 0 <= i - j < taps else nothing for j in range(2)]
                pair = jnp.concatenate(pair, axis=1)
                at = lax.rem(i + 2 * lower, rows) + a * rows
                packed[pl.ds(pl.multiple_of(at * width, width), width), across] = pair


def first_layer(tile, frames, packed, bias):
    taps = 3
    rows = taps + 1
    left = jnp.concatenate(
        [
            jnp.concatenate([tile(f + a, k) for f in frames], axis=0)
            for a in range(taps)
            for k in range(rows)
        ],
        axis=1,
    )
    double = packed.shape[1] // taps
    columns = left.shape[0] // len(frames)
    part = lambda e: jnp.dot(left, packed[:, e * double : (e + 1) * double], preferred_element_type=jnp.float32)
    return silu(shifted_sum(part, columns) + bias).astype(jnp.bfloat16)


def second_layer(terms, second):
    left = jnp.concatenate([tile for tile, _, _ in terms], axis=1)

    def part(e):
        right = jnp.concatenate([second[a, b, e] for _, a, b in terms], axis=0)
        return jnp.dot(left, right, preferred_element_type=jnp.float32)

    return shifted_sum(part, left.shape[0])


def terms_of(tile, frames, late):
    both = [(tile(n, j), a, 1 - late + j) for n, a in frames for j in range(2)]
    return both, [(tile(n, late), a, 2 * (1 - late)) for n, a in frames]


def put_rows(result, target, start, columns, masks):
    width = target.shape[-1]
    for n in range(result.shape[0] // columns):
        for j in range(2):
            row = result[n * columns : (n + 1) * columns, j * width : (j + 1) * width]
            target[start + n, j] = row if masks is None else jnp.where(masks[j], row, jnp.zeros_like(row))


def border_masks():
    lower, known = lower_half(), border_known()
    return [known | (lower != j) for j in range(2)]


def last_slab():
    return lax.axis_index("slab") == lax.axis_size("slab") - 1


def masked(row, *conditions):
    for condition in conditions:
        row = jnp.where(condition, row, jnp.zeros_like(row))
    return row


def ahead_kernel(*refs, border):
    early_first, late_first, early_second, late_second, packed, bias, hidden, *sent = refs
    early, half, columns = early_first.shape[:3]
    ahead = late_second.shape[0] - early
    unknown = [border_known()] if border else []

    def tile(f, k):
        first, second = (early_first, early_second) if f < early else (late_first, late_second)
        return masked(first[f % early, k], *unknown) if k < half else second[f % early + (ahead if f >= early else 0), k - half]

    @pl.when(jnp.logical_not(last_slab()))
    def _():
        result = first_layer(tile, range(hidden.shape[0]), packed, bias[...])
        put_rows(result, hidden, 0, columns, border_masks() if border else None)
        for target in sent:
            size = target.shape[0] - SPARE
            target[:size] = hidden[...].reshape(size, target.shape[1])
            target[size:] = jnp.zeros((SPARE, target.shape[1]), target.dtype)

    @pl.when(last_slab())
    def _():
        for target in (hidden, *sent):
            target[...] = jnp.zeros(target.shape, target.dtype)


def behind(first, second, passed_first, passed_second, packed, bias, ahead, hidden, border):
    early, half, columns = passed_first.shape[:3]
    follows = lax.axis_index("slab") > 0
    unknown = [border_known()] if border else []

    def tile(f, k):
        if f >= early:
            part = (first if k < half else second)[f // early - 1]
            at = f % early + (part.shape[0] - early if f >= 2 * early else 0)
            return masked(part[at, k % half], *(unknown if k < half else []))
        if k < half:
            return masked(passed_first[f, k], follows, *unknown)
        return masked(passed_second[f, k - half], follows)

    def fill(frames):
        result = first_layer(tile, range(frames), packed, bias[...])
        put_rows(result, hidden, 0, columns, border_masks() if border else None)

    @pl.when(jnp.logical_not(last_slab()))
    def _():
        fill(early)
        hidden[early] = ahead[0]

    pl.when(last_slab())(lambda: fill(early + 1))


def inner_kernel(
    front, late, rest_front, rest_late, passed, passed_other, packed, bias, ahead, second, partial, hidden
):
    halves = (front, late), (rest_front, rest_late)
    behind(*halves, passed, passed_other, packed, bias, ahead, hidden, False)

    def store(t, row, value):
        partial[t, row] = value

    add_layers(hidden, lower_half(), second, store)


def add_layers(hidden, late, second, store):
    tile = lambda n, j: hidden[n, j]
    for t, frames in enumerate(([(0, 2)], [(0, 0), (1, 1), (2, 2)])):
        for row, terms in zip((1 - late, late), terms_of(tile, frames, late)):
            store(t, row, second_layer(terms, second))


def finish(value, bias, row, kept, given):
    core = lax.axis_index("chan")
    total = silu(value + bias[...]).astype(jnp.bfloat16)
    portion = kept.shape[-1]
    low, high = total[:, :portion], total[:, portion:]
    kept[row] = jnp.where(core == 0, low, high)
    given[row] = jnp.where(core == 0, high, low)


def outer_kernel(
    front, late, beyond_front, beyond_late, passed, passed_beyond, packed, bias, ahead, second, bias_second, partial,
    kept, given, left, hidden,
):
    halves = (beyond_front, beyond_late), (front, late)
    behind(*halves, passed_beyond, passed, packed, bias, ahead, hidden, True)

    def store(t, row, value):
        if t == 0:
            left[row] = partial[t, row] + value
        else:
            finish(partial[t, row] + value, bias_second, row, kept, given)

    add_layers(hidden, 1 - lower_half(), second, store)


def last_kernel(
    handed_inner, handed_outer, second, bias_second, left, kept, given
):
    lower = lower_half()
    follows = lax.axis_index("slab") > 0
    frames = [(0, 0), (1, 1)]

    @pl.when(follows)
    def _():
        half, columns = handed_outer.shape[1:3]

        def inner(n, j):
            return handed_inner[pl.ds(pl.multiple_of((n * half + j) * columns, columns), columns)]

        inner_both, inner_one = terms_of(inner, frames, lower)
        outer_both, outer_one = terms_of(lambda n, j: handed_outer[n, j], frames, 1 - lower)
        for row, terms in ((1 - lower, inner_both + outer_one), (lower, outer_both + inner_one)):
            finish(left[row] + second_layer(terms, second), bias_second, row, kept, given)

    @pl.when(jnp.logical_not(follows))
    def _():
        for row in range(left.shape[0]):
            finish(left[row], bias_second, row, kept, given)


def cycle(value, axis):
    count = lax.axis_size(axis)
    return lax.ppermute(value, axis, [(i, (i + 1) % count) for i in range(count)])


def across_border(value):
    clips, tiles = lax.axis_size("clip"), lax.axis_size("tile")
    at = lambda c, t, k: (c * tiles + t) * 2 + k
    pairs = []
    for clip in range(clips):
        for tile in range(tiles - 1):
            core = (tile + 1) % 2
            pairs.append((at(clip, tile, core), at(clip, tile + 1, core)))
            pairs.append((at(clip, tile + 1, core), at(clip, tile, core)))
        if clips > 1:
            for tile, core in ((0, 0), (tiles - 1, tiles % 2)):
                pairs.append((at(clip, tile, core), at((clip + 1) % clips, tile, core)))
    return lax.ppermute(value, ("clip", "tile", "chan"), pairs)


def shards(video, first_weight, first_bias, second_weight, second_bias):
    frames, rows, columns, width = video.shape
    half = rows // 2
    taps = first_weight.shape[0]
    assert half == taps - 1 and frames == 2 * (taps - 1) and lax.axis_size("chan") == 2
    bf16 = jnp.bfloat16
    shape = jax.ShapeDtypeStruct
    small = pl.CostEstimate(flops=1000, bytes_accessed=1000, transcendentals=0)

    def call(kernel, outs, ins, scratch, *operands, out_specs=None, limit=LIMIT):
        return pl.pallas_call(
            kernel,
            out_shape=outs,
            in_specs=ins,
            out_specs=[VMEM] * len(outs) if out_specs is None else out_specs,
            scratch_shapes=scratch,
            compiler_params=pltpu.CompilerParams(vmem_limit_bytes=limit),
            cost_estimate=small,
        )(*operands)

    early = frames // 2
    short = shape((early, half, columns, width), bf16)
    turned = jnp.swapaxes(first_weight, 3, 4).reshape(-1, width)
    far = lambda value: pltpu.with_memory_space_constraint(value, pltpu.HBM)
    front, late, rest, staged = call(
        stage_kernel,
        [
            pltpu.VMEM(short.shape, bf16),
            pltpu.VMEM(short.shape, bf16),
            pltpu.VMEM((frames,) + short.shape[1:], bf16),
            pltpu.VMEM((turned.shape[0] + TAIL, width), bf16),
        ],
        [HBM] * 4,
        [
            pltpu.VMEM((1, first_bias.shape[0]), jnp.float32),
            pltpu.VMEM((1, second_bias.shape[0]), jnp.float32),
            pltpu.SemaphoreType.DMA((6,)),
        ],
        far(video), far(turned), far(first_bias.reshape(1, -1)), far(second_bias.reshape(1, -1)),
    )
    beyond_front, beyond_late = across_border(front), across_border(late)
    passed = cycle(late, "slab")
    staged_other = cycle(staged, "chan")
    matrix = shape((taps * (taps + 1) * width, taps * 2 * width), bf16)
    channels = second_weight.shape[4]
    packed, bias_first, bias_last = call(
        pack_kernel,
        [matrix, shape((1, 2 * width), jnp.float32), shape((1, channels), jnp.float32)],
        [VMEM] * 2,
        [],
        staged, staged_other,
    )
    ahead_inner, sent = call(
        functools.partial(ahead_kernel, border=False),
        [short, shape((early * half * columns + SPARE, width), bf16)],
        [VMEM] * 6, [], front, late, rest, rest,
        packed, bias_first
    )
    handed_inner = cycle(sent, "slab")
    passed, _ = lax.optimization_barrier((passed, ahead_inner))
    passed_other = cycle(passed, "chan")
    passed_beyond = across_border(passed)
    (ahead_outer,) = call(
        functools.partial(ahead_kernel, border=True),
        [short],
        [VMEM] * 6,
        [],
        beyond_front, beyond_late, front, late, packed, bias_first,
    )
    handed_outer = cycle(ahead_outer, "slab")
    (partial,) = call(
        inner_kernel,
        [shape((early, half, columns, channels), jnp.float32)],
        [VMEM] * 10,
        [pltpu.VMEM((early + 1, half, columns, width), bf16)],
        front, late, rest, rest, passed, passed_other, packed, bias_first, ahead_inner, second_weight,
    )
    part = shape((half, columns, second_bias.shape[0]), bf16)
    handed_inner, partial = lax.optimization_barrier((handed_inner, partial))
    kept_second, given_second, left = call(
        outer_kernel,
        [part, part, shape((half, columns, channels), jnp.float32)],
        [VMEM] * 12,
        [pltpu.VMEM((early + 1, half, columns, width), bf16)],
        front, late, beyond_front, beyond_late, passed, passed_beyond, packed, bias_first, ahead_outer, second_weight, bias_last, partial,
    )
    taken_second = cycle(given_second, "chan")
    left, taken_second = lax.optimization_barrier((left, taken_second))
    kept_first, given_first = call(
        last_kernel, [part, part], [VMEM] * 5, [], handed_inner, handed_outer, second_weight, bias_last, left
    )
    (latents,) = call(
        join_kernel,
        [shape((early, rows, columns, second_bias.shape[0]), bf16)],
        [VMEM] * 4,
        [pltpu.SemaphoreType.DMA((4,))],
        kept_first, cycle(given_first, "chan"), kept_second, taken_second,
        out_specs=[ANY],
    )
    return latents


def solution(mesh):
    placed = (
        P(("clip", "slab"), "tile", None, None),
        P(None, None, None, None, "chan"),
        P("chan"),
        P(),
        P("chan"),
    )
    return jax.shard_map(
        shards,
        mesh=mesh,
        in_specs=placed,
        out_specs=P(("clip", "slab"), "tile", None, "chan"),
        check_vma=False,
    )
```

```python
import functools

import jax
import jax.numpy as jnp
from jax import lax
from jax.experimental import pallas as pl
from jax.experimental.pallas import tpu as pltpu
from jax.sharding import PartitionSpec as P

VMEM = pl.BlockSpec(memory_space=pltpu.VMEM)
ANY = pl.BlockSpec(memory_space=pl.ANY)
HBM = pl.BlockSpec(memory_space=pltpu.HBM)
LIMIT = 20 * 1024 * 1024
TAIL = 16
SPARE = 16


def silu(value):
    half = 0.5 * value
    return half + half * jnp.tanh(half)


def shifted_sum(part, columns):
    def cells(value):
        size, width = value.shape
        value = value.reshape(size // columns, columns, width)
        return value, lax.broadcasted_iota(jnp.int32, (1, columns, width), 1)

    before, cell = cells(part(0))
    total = jnp.where(cell == 0, 0.0, pltpu.roll(before, 1, 1))
    after, cell = cells(part(2))
    total = total + jnp.where(cell == columns - 1, 0.0, pltpu.roll(after, columns - 1, 1))
    here = part(1)
    return here + total.reshape(here.shape)


def lower_half():
    return lax.rem(lax.axis_index("chan") + lax.axis_index("tile"), 2)


def border_known():
    lower, tile = lower_half(), lax.axis_index("tile")
    last = lax.axis_size("tile") - 1
    return jnp.logical_not(jnp.logical_or((lower == 0) & (tile == 0), (lower == 1) & (tile == last)))


def thirds(value):
    high = value.astype(jnp.bfloat16)
    left = value - high.astype(jnp.float32)
    middle = left.astype(jnp.bfloat16)
    return [high, middle, (left - middle.astype(jnp.float32)).astype(jnp.bfloat16)]


def stage_kernel(video, weight, first_bias, second_bias, front, late, rest_front, rest_late, staged, first_line, second_line, sems):
    lower = lower_half()
    early, half = front.shape[:2]
    size = weight.shape[0]
    pairs = (
        (first_bias, first_line),
        (second_bias, second_line),
        (video.at[early:, pl.ds(lower * half, half)], late),
        (video.at[:early, pl.ds(lower * half, half)], front),
        (video.at[early:, pl.ds((1 - lower) * half, half)], rest_late),
        (video.at[:early, pl.ds((1 - lower) * half, half)], rest_front),
        (weight, staged.at[0:size]),
    )
    copies = [pltpu.make_async_copy(source, target, sems.at[k]) for k, (source, target) in enumerate(pairs)]
    for copy in copies:
        copy.start()
    for copy in copies[:2]:
        copy.wait()
    width = staged.shape[1]
    first = first_line[...]
    first = jnp.concatenate([first, jnp.zeros((1, width - first.shape[1]), first.dtype)], axis=1)
    rows = thirds(first) + thirds(second_line[...])
    rows.append(jnp.zeros((TAIL - len(rows), width), jnp.bfloat16))
    staged[size:] = jnp.concatenate(rows, axis=0)
    for copy in copies[2:]:
        copy.wait()


def join_kernel(*refs):
    *parts, latents, sems = refs
    lower = lower_half()
    half = parts[0].shape[0]
    copies = []
    for k, part in enumerate(parts):
        place = lower if k % 2 == 0 else 1 - lower
        copies.append(pltpu.make_async_copy(part, latents.at[k // 2, pl.ds(place * half, half)], sems.at[k]))
    for copy in copies:
        copy.start()
    for copy in copies:
        copy.wait()


def pack_kernel(own, other, packed, bias_first, bias_second):
    core, lower = lax.axis_index("chan"), lower_half()
    taps = 3
    rows = taps + 1
    width = own.shape[1]
    size = own.shape[0] - TAIL
    channels = size // taps**3

    def lines(source):
        last = source[size:].astype(jnp.float32)
        added = [last[3 * k : 3 * k + 1] + last[3 * k + 1 : 3 * k + 2] + last[3 * k + 2 : 3 * k + 3] for k in range(2)]
        return added[0][:, :channels], added[1]

    mine, theirs = lines(own), lines(other)
    low = [jnp.where(core == 0, m, t) for m, t in zip(mine, theirs)]
    high = [jnp.where(core == 0, t, m) for m, t in zip(mine, theirs)]
    once = jnp.concatenate([low[0], high[0]], axis=1)
    bias_first[...] = jnp.concatenate([once, once], axis=1)
    bias_second[...] = jnp.concatenate([low[1], high[1]], axis=1)
    for a in range(taps):
        for e in range(taps):
            full = []
            for b in range(taps):
                at = ((a * taps + b) * taps + e) * channels
                mine, theirs = own[at : at + channels], other[at : at + channels]
                low = jnp.where(core == 0, mine, theirs)
                high = jnp.where(core == 0, theirs, mine)
                full.append(jnp.concatenate([low, high], axis=0).T)
            nothing = jnp.zeros_like(full[0])
            across = slice(e * 2 * width, (e + 1) * 2 * width)
            for i in range(rows):
                pair = [full[i - j] if 0 <= i - j < taps else nothing for j in range(2)]
                pair = jnp.concatenate(pair, axis=1)
                at = lax.rem(i + 2 * lower, rows) + a * rows
                packed[pl.ds(pl.multiple_of(at * width, width), width), across] = pair


def first_layer(tile, frames, packed, bias):
    taps = 3
    rows = taps + 1
    left = jnp.concatenate(
        [
            jnp.concatenate([tile(f + a, k) for f in frames], axis=0)
            for a in range(taps)
            for k in range(rows)
        ],
        axis=1,
    )
    double = packed.shape[1] // taps
    columns = left.shape[0] // len(frames)
    part = lambda e: jnp.dot(left, packed[:, e * double : (e + 1) * double], preferred_element_type=jnp.float32)
    return silu(shifted_sum(part, columns) + bias).astype(jnp.bfloat16)


def second_layer(terms, second):
    left = jnp.concatenate([tile for tile, _, _ in terms], axis=1)

    def part(e):
        right = jnp.concatenate([second[a, b, e] for _, a, b in terms], axis=0)
        return jnp.dot(left, right, preferred_element_type=jnp.float32)

    return shifted_sum(part, left.shape[0])


def terms_of(tile, frames, late):
    both = [(tile(n, j), a, 1 - late + j) for n, a in frames for j in range(2)]
    return both, [(tile(n, late), a, 2 * (1 - late)) for n, a in frames]


def put_rows(result, target, start, columns, masks):
    width = target.shape[-1]
    for n in range(result.shape[0] // columns):
        for j in range(2):
            row = result[n * columns : (n + 1) * columns, j * width : (j + 1) * width]
            target[start + n, j] = row if masks is None else jnp.where(masks[j], row, jnp.zeros_like(row))


def border_masks():
    lower, known = lower_half(), border_known()
    return [known | (lower != j) for j in range(2)]


def last_slab():
    return lax.axis_index("slab") == lax.axis_size("slab") - 1


def masked(row, *conditions):
    for condition in conditions:
        row = jnp.where(condition, row, jnp.zeros_like(row))
    return row


def ahead_kernel(*refs, border):
    early_first, late_first, early_second, late_second, packed, bias, hidden, *sent = refs
    early, half, columns = early_first.shape[:3]
    unknown = [border_known()] if border else []

    def tile(f, k):
        first, second = (early_first, early_second) if f < early else (late_first, late_second)
        return masked(first[f % early, k], *unknown) if k < half else second[f % early, k - half]

    @pl.when(jnp.logical_not(last_slab()))
    def _():
        result = first_layer(tile, range(hidden.shape[0]), packed, bias[...])
        put_rows(result, hidden, 0, columns, border_masks() if border else None)
        for target in sent:
            size = target.shape[0] - SPARE
            target[:size] = hidden[...].reshape(size, target.shape[1])
            target[size:] = jnp.zeros((SPARE, target.shape[1]), target.dtype)

    @pl.when(last_slab())
    def _():
        for target in (hidden, *sent):
            target[...] = jnp.zeros(target.shape, target.dtype)


def behind(first, second, passed_first, passed_second, packed, bias, ahead, hidden, border):
    early, half, columns = passed_first.shape[:3]
    follows = lax.axis_index("slab") > 0
    unknown = [border_known()] if border else []

    def tile(f, k):
        if f >= early:
            part = (first if k < half else second)[f // early - 1]
            return masked(part[f % early, k % half], *(unknown if k < half else []))
        if k < half:
            return masked(passed_first[f, k], follows, *unknown)
        return masked(passed_second[f, k - half], follows)

    def fill(frames):
        result = first_layer(tile, range(frames), packed, bias[...])
        put_rows(result, hidden, 0, columns, border_masks() if border else None)

    @pl.when(jnp.logical_not(last_slab()))
    def _():
        fill(early)
        hidden[early] = ahead[0]

    pl.when(last_slab())(lambda: fill(early + 1))


def inner_kernel(
    front, late, rest_front, rest_late, passed, passed_other, packed, bias, ahead, second, partial, hidden
):
    halves = (front, late), (rest_front, rest_late)
    behind(*halves, passed, passed_other, packed, bias, ahead, hidden, False)

    def store(t, row, value):
        partial[t, row] = value

    add_layers(hidden, lower_half(), second, store)


def add_layers(hidden, late, second, store):
    tile = lambda n, j: hidden[n, j]
    for t, frames in enumerate(([(0, 2)], [(0, 0), (1, 1), (2, 2)])):
        for row, terms in zip((1 - late, late), terms_of(tile, frames, late)):
            store(t, row, second_layer(terms, second))


def finish(value, bias, row, kept, given):
    core = lax.axis_index("chan")
    total = silu(value + bias[...]).astype(jnp.bfloat16)
    portion = kept.shape[-1]
    low, high = total[:, :portion], total[:, portion:]
    kept[row] = jnp.where(core == 0, low, high)
    given[row] = jnp.where(core == 0, high, low)


def outer_kernel(
    front, late, beyond_front, beyond_late, passed, passed_beyond, packed, bias, ahead, second, bias_second, partial,
    kept, given, left, hidden,
):
    halves = (beyond_front, beyond_late), (front, late)
    behind(*halves, passed_beyond, passed, packed, bias, ahead, hidden, True)

    def store(t, row, value):
        if t == 0:
            left[row] = partial[t, row] + value
        else:
            finish(partial[t, row] + value, bias_second, row, kept, given)

    add_layers(hidden, 1 - lower_half(), second, store)


def last_kernel(
    handed_inner, handed_outer, second, bias_second, left, kept, given
):
    lower = lower_half()
    follows = lax.axis_index("slab") > 0
    frames = [(0, 0), (1, 1)]

    @pl.when(follows)
    def _():
        half, columns = handed_outer.shape[1:3]

        def inner(n, j):
            return handed_inner[pl.ds(pl.multiple_of((n * half + j) * columns, columns), columns)]

        inner_both, inner_one = terms_of(inner, frames, lower)
        outer_both, outer_one = terms_of(lambda n, j: handed_outer[n, j], frames, 1 - lower)
        for row, terms in ((1 - lower, inner_both + outer_one), (lower, outer_both + inner_one)):
            finish(left[row] + second_layer(terms, second), bias_second, row, kept, given)

    @pl.when(jnp.logical_not(follows))
    def _():
        for row in range(left.shape[0]):
            finish(left[row], bias_second, row, kept, given)


def cycle(value, axis):
    count = lax.axis_size(axis)
    return lax.ppermute(value, axis, [(i, (i + 1) % count) for i in range(count)])


def across_border(value):
    clips, tiles = lax.axis_size("clip"), lax.axis_size("tile")
    at = lambda c, t, k: (c * tiles + t) * 2 + k
    pairs = []
    for clip in range(clips):
        for tile in range(tiles - 1):
            core = (tile + 1) % 2
            pairs.append((at(clip, tile, core), at(clip, tile + 1, core)))
            pairs.append((at(clip, tile + 1, core), at(clip, tile, core)))
        if clips > 1:
            for tile, core in ((0, 0), (tiles - 1, tiles % 2)):
                pairs.append((at(clip, tile, core), at((clip + 1) % clips, tile, core)))
    return lax.ppermute(value, ("clip", "tile", "chan"), pairs)


def shards(video, first_weight, first_bias, second_weight, second_bias):
    frames, rows, columns, width = video.shape
    half = rows // 2
    taps = first_weight.shape[0]
    assert half == taps - 1 and frames == 2 * (taps - 1) and lax.axis_size("chan") == 2
    bf16 = jnp.bfloat16
    shape = jax.ShapeDtypeStruct
    small = pl.CostEstimate(flops=1000, bytes_accessed=1000, transcendentals=0)

    def call(kernel, outs, ins, scratch, *operands, out_specs=None, limit=LIMIT):
        return pl.pallas_call(
            kernel,
            out_shape=outs,
            in_specs=ins,
            out_specs=[VMEM] * len(outs) if out_specs is None else out_specs,
            scratch_shapes=scratch,
            compiler_params=pltpu.CompilerParams(vmem_limit_bytes=limit),
            cost_estimate=small,
        )(*operands)

    early = frames // 2
    short = shape((early, half, columns, width), bf16)
    turned = jnp.swapaxes(first_weight, 3, 4).reshape(-1, width)
    far = lambda value: pltpu.with_memory_space_constraint(value, pltpu.HBM)
    front, late, rest_front, rest_late, staged = call(
        stage_kernel,
        [
            pltpu.VMEM(short.shape, bf16),
            pltpu.VMEM(short.shape, bf16),
            pltpu.VMEM(short.shape, bf16),
            pltpu.VMEM(short.shape, bf16),
            pltpu.VMEM((turned.shape[0] + TAIL, width), bf16),
        ],
        [HBM] * 4,
        [
            pltpu.VMEM((1, first_bias.shape[0]), jnp.float32),
            pltpu.VMEM((1, second_bias.shape[0]), jnp.float32),
            pltpu.SemaphoreType.DMA((7,)),
        ],
        far(video), far(turned), far(first_bias.reshape(1, -1)), far(second_bias.reshape(1, -1)),
    )
    beyond_front, beyond_late = across_border(front), across_border(late)
    passed = cycle(late, "slab")
    staged_other = cycle(staged, "chan")
    matrix = shape((taps * (taps + 1) * width, taps * 2 * width), bf16)
    channels = second_weight.shape[4]
    packed, bias_first, bias_last = call(
        pack_kernel,
        [matrix, shape((1, 2 * width), jnp.float32), shape((1, channels), jnp.float32)],
        [VMEM] * 2,
        [],
        staged, staged_other,
    )
    ahead_inner, sent = call(
        functools.partial(ahead_kernel, border=False),
        [short, shape((early * half * columns + SPARE, width), bf16)],
        [VMEM] * 6, [], front, late, rest_front, rest_late,
        packed, bias_first
    )
    handed_inner = cycle(sent, "slab")
    passed, _ = lax.optimization_barrier((passed, ahead_inner))
    passed_other = cycle(passed, "chan")
    passed_beyond = across_border(passed)
    (ahead_outer,) = call(
        functools.partial(ahead_kernel, border=True),
        [short],
        [VMEM] * 6,
        [],
        beyond_front, beyond_late, front, late, packed, bias_first,
    )
    handed_outer = cycle(ahead_outer, "slab")
    (partial,) = call(
        inner_kernel,
        [shape((early, half, columns, channels), jnp.float32)],
        [VMEM] * 10,
        [pltpu.VMEM((early + 1, half, columns, width), bf16)],
        front, late, rest_front, rest_late, passed, passed_other, packed, bias_first, ahead_inner, second_weight,
    )
    part = shape((half, columns, second_bias.shape[0]), bf16)
    handed_inner, partial = lax.optimization_barrier((handed_inner, partial))
    kept_second, given_second, left = call(
        outer_kernel,
        [part, part, shape((half, columns, channels), jnp.float32)],
        [VMEM] * 12,
        [pltpu.VMEM((early + 1, half, columns, width), bf16)],
        front, late, beyond_front, beyond_late, passed, passed_beyond, packed, bias_first, ahead_outer, second_weight, bias_last, partial,
    )
    taken_second = cycle(given_second, "chan")
    left, taken_second = lax.optimization_barrier((left, taken_second))
    kept_first, given_first = call(
        last_kernel, [part, part], [VMEM] * 5, [], handed_inner, handed_outer, second_weight, bias_last, left
    )
    (latents,) = call(
        join_kernel,
        [shape((early, rows, columns, second_bias.shape[0]), bf16)],
        [VMEM] * 4,
        [pltpu.SemaphoreType.DMA((4,))],
        kept_first, cycle(given_first, "chan"), kept_second, taken_second,
        out_specs=[ANY],
    )
    return latents


def solution(mesh):
    placed = (
        P(("clip", "slab"), "tile", None, None),
        P(None, None, None, None, "chan"),
        P("chan"),
        P(),
        P("chan"),
    )
    return jax.shard_map(
        shards,
        mesh=mesh,
        in_specs=placed,
        out_specs=P(("clip", "slab"), "tile", None, "chan"),
        check_vma=False,
    )
```
